256 devices in a mesh: sp: 32 (over z, y), cp: 8 (over x, core).
Axes of the slice: x: 4, y: 4, z: 8, core: 2. Of those that a mesh axis runs over, the one named last changes fastest.
Arguments:
- queries: bfloat16 [32768, 4096], P(('cp', 'sp')), may hold values from -80 to 80
- keyvals: bfloat16 [32768, 4, 256], P(('cp', 'sp')), may hold values from -8 to 8
- residual: bfloat16 [32768, 2048], P(('cp', 'sp')), may hold values from -3 to 3
- out_weight: bfloat16 [4096, 2048], P('cp'), may hold values from -0.09375 to 0.09375
- norm_gain: float32 [2048], replicated, may hold values from 0.5 to 2
- doc_ids: int32 [32768], replicated, may hold values from 0 to 63, never falling along the last dimension, each value on 1 to 1024 neighbouring positions
- expert_ids: int32 [32768, 8], P(('cp', 'sp')), may hold values from 0 to 127, all different within a row
- route_weights: float32 [32768, 8], P(('cp', 'sp')), may hold values from 0.05 to 0.5
- expert_in: bfloat16 [256, 2048, 768], P(('sp', 'cp')), may hold values from -0.125 to 0.125
- expert_out: bfloat16 [256, 384, 2048], P(('sp', 'cp')), may hold values from -0.21875 to 0.21875
Outputs:
- mixed: bfloat16 [32768, 2048], P(('cp', 'sp'))
The draws below stay inside these ranges and needn't reach their ends.
Inputs may be any that keep to these rules, and one draw needn't show every extreme that they name: `doc_ids`: document numbers never fall along the positions, and a document holds at most 1024 positions. `expert_ids`: each token names 8 different experts.
All inputs are finite; a program needn't handle non-finite values.
Results may differ from the reference program's by a relative error of at most 0.022.
Values may be sent and summed in bfloat16 or wider, within the bound.
A program may use at most 128 MiB of HBM per device.

```python
import math
import jax
import jax.numpy as jnp
import numpy as np
from jax import lax

D = 2048
HEADS = 32
KVH = 4
HD = 128
FF_E = 768
TOP = 8
TOK_DEV = 128
EXPERTS = 128
PARTS_SIZE = 2
TOKENS = 32768
DOC_MAX = 1024
DOCS = 64
CAP = 8
HG = 4
BLOCK = 512
N_SP = 32
N_CP = 8


def shared_keys(key):
    sub_key = jax.random.fold_in(key, 11)
    return jnp.clip(jax.random.normal(sub_key, (TOKENS, KVH, HD), jnp.float32), -4.0, 4.0)


def draw_keyvals(key, part):
    base_keys = shared_keys(key)
    key = jax.random.fold_in(key, 3)
    values = jnp.clip(jax.random.normal(key, (TOKENS, KVH, HD), jnp.float32), -4.0, 4.0)
    return jnp.concatenate([base_keys, values], axis=-1).astype(jnp.bfloat16)


def draw_queries(key, part):
    key = jax.random.fold_in(key, 4)
    noise_rows = jnp.clip(jax.random.normal(key, (TOKENS, HEADS, HD), jnp.float32), -4.0, 4.0)
    return noise_rows.reshape(TOKENS, HEADS * HD).astype(jnp.bfloat16)


def steps_of(stream_key, dims, shards, low, top_value):
    gain, own = 1.0, jax.random.fold_in(stream_key, 6)
    for position, blocks in shards:
        heights = jnp.exp(jax.random.uniform(jax.random.fold_in(own, position), (blocks,), jnp.float32, low / len(shards), top_value / len(shards)))
        gain = gain * jnp.repeat(heights, dims[position] // blocks).reshape([-1 if axis == position else 1 for axis in range(len(dims))])
    return gain


def different_ones(key, rows, amount, top, lift):
    ranking = jax.random.permutation(jax.random.fold_in(key, 1), amount)
    favour = ranking
    for power in range(3):
        favour = favour * favour // amount
    favour = favour * lift // amount
    lots = jax.random.randint(jax.random.fold_in(key, 2), (rows, amount), 0, 4096) + favour
    fixed_rows = jax.random.permutation(jax.random.fold_in(key, 3), rows)[jnp.arange(amount) % rows]
    lots = jnp.where(jnp.arange(rows)[:, None] == fixed_rows[None, :], 1 << 14, lots)
    score = lots * amount + jnp.arange(amount)
    return lax.top_k(score.astype(jnp.int32), top)[1].astype(jnp.int32)


def split_up(amount, total, limit, slope):
    weights = [(1 << 20) // math.isqrt(rank ** slope) + 1 for rank in range(2, amount + 1)]
    spare, given = total - limit - (amount - 1), [1] * (amount - 1)
    while spare > 0:
        free = [i for i in range(amount - 1) if given[i] < limit]
        whole, remaining = sum([weights[i] for i in free]), spare
        for i in free:
            addition = min(limit - given[i], max(1, remaining * weights[i] // whole), spare)
            given[i] = given[i] + addition
            spare = spare - addition
    return np.array([limit] + given)


def ragged_sizes(own_key, amount, total, bound, lean):
    if amount == 2:
        one = jax.random.randint(own_key, (), max(1, total - bound), min(bound, total - 1) + 1)
        return jnp.stack([one, total - one])
    lengths = jnp.asarray(split_up(amount, total, bound, lean), jnp.int32)
    pairs = (amount - 1) // 2
    source_of, sink = lengths[1:1 + 2 * pairs:2], lengths[2:2 + 2 * pairs:2]
    room = jnp.minimum(source_of - 1, bound - sink)
    moved = jax.random.randint(jax.random.fold_in(own_key, 1), (pairs,), 0, 1 << 20) % (room + 1)
    lengths = lengths.at[1:1 + 2 * pairs:2].set(source_of - moved).at[2:2 + 2 * pairs:2].set(sink + moved)
    return lengths[jax.random.permutation(jax.random.fold_in(own_key, 2), amount)]


def bell_draw(own_key, dims, scale, bound, split=(), kind=jnp.bfloat16):
    result = jax.random.normal(own_key, dims, jnp.float32) * scale
    if len(split) > 0:
        result = steps_of(own_key, dims, split, -0.22, 0.18) * result
    return jnp.clip(result, min=-bound, max=bound).astype(kind)


def setup_inputs(seed: int = 0) -> dict:
    seeds = jax.random.split(jax.random.key(seed), 11)
    return {
        "queries": draw_queries(jax.random.fold_in(seeds[10], 71), 0),
        "keyvals": draw_keyvals(jax.random.fold_in(seeds[10], 71), 0),
        "residual": bell_draw(seeds[2], (TOKENS, D), 0.5, 3.0, ((0, 256),)),
        "out_weight": bell_draw(seeds[3], (HEADS * HD, D), (HEADS * HD) ** -0.5, 0.09375, ((0, 8),)),
        "norm_gain": jnp.clip(jnp.exp(jax.random.uniform(seeds[4], (D,), jnp.float32, math.log(0.5), math.log(2.0))), 0.5, 2.0),
        "doc_ids": jnp.searchsorted(jnp.cumsum(ragged_sizes(seeds[5], DOCS, TOKENS, DOC_MAX, 1)), jnp.arange(TOKENS), side="right").astype(jnp.int32),
        "expert_ids": different_ones(seeds[6], TOKENS, EXPERTS, TOP, 512),
        "route_weights": jnp.clip(jnp.exp(math.log(0.5) - 2.3025851 * jax.random.uniform(seeds[7], (TOKENS, TOP), jnp.float32) ** steps_of(seeds[7], (TOKENS, TOP), ((0, 256),), -0.2, 0.2)), 0.05, 0.5),
        "expert_in": bell_draw(seeds[8], (EXPERTS * PARTS_SIZE, D, 2 * FF_E // PARTS_SIZE), D ** -0.5, 0.125, ((0, 256),)),
        "expert_out": bell_draw(seeds[9], (EXPERTS * PARTS_SIZE, FF_E // PARTS_SIZE, D), FF_E ** -0.5, 0.21875, ((0, 256),)),
    }


def reference(queries, keyvals, residual, out_weight, norm_gain, doc_ids, expert_ids, route_weights, expert_in, expert_out):
    group_size = HEADS // KVH
    window = DOC_MAX + BLOCK
    score_scale = 1.0 / math.sqrt(HD)
    q_all = queries.reshape(TOKENS, HEADS, HD)
    keys_padded = jnp.concatenate([jnp.zeros((DOC_MAX, KVH, 2 * HD), jnp.bfloat16), keyvals], axis=0)
    docs_padded = jnp.concatenate([jnp.full((DOC_MAX,), -1, jnp.int32), doc_ids], axis=0)

    def one_block(block_num):
        first_row = block_num * BLOCK
        q_block = lax.dynamic_slice_in_dim(q_all, first_row, BLOCK, 0).astype(jnp.float32)
        k_block = lax.dynamic_slice_in_dim(keys_padded, first_row, window, 0)
        k_block = jnp.repeat(k_block, group_size, axis=1).astype(jnp.float32)
        q_docs = lax.dynamic_slice_in_dim(doc_ids, first_row, BLOCK, 0)
        k_docs = lax.dynamic_slice_in_dim(docs_padded, first_row, window, 0)
        q_pos = first_row + jnp.arange(BLOCK, dtype=jnp.int32)
        k_pos = first_row - DOC_MAX + jnp.arange(window, dtype=jnp.int32)
        allowed = (k_docs[None, :] == q_docs[:, None]) & (k_pos[None, :] <= q_pos[:, None])
        scores = jnp.einsum('bhd,khd->hbk', q_block, k_block[:, :, :HD]) * score_scale
        scores = jnp.where(allowed[None], scores, jnp.float32(-1e+30))
        row_max = lax.optimization_barrier(jnp.max(scores, axis=-1, keepdims=True))
        exponent = jnp.exp(scores - row_max)
        denominator = lax.optimization_barrier(jnp.sum(exponent, axis=-1))
        weights_bf = lax.optimization_barrier(exponent.astype(jnp.bfloat16))
        numerator = jnp.einsum('hbk,khd->bhd', weights_bf.astype(jnp.float32), k_block[:, :, HD:])
        return (numerator / jnp.transpose(denominator)[:, :, None]).astype(jnp.bfloat16)
    attended = lax.map(one_block, jnp.arange(TOKENS // BLOCK, dtype=jnp.int32)).reshape(TOKENS, HEADS * HD)
    projected = jnp.zeros((TOKENS, D), jnp.float32)
    group_cols = HG * HD
    for group_num in range(N_CP):
        share = jnp.dot(attended[:, group_num * group_cols:(group_num + 1) * group_cols], out_weight[group_num * group_cols:(group_num + 1) * group_cols], preferred_element_type=jnp.float32)
        share = lax.optimization_barrier(share.astype(jnp.bfloat16))
        projected = projected + share.astype(jnp.float32)
    summed = residual.astype(jnp.float32) + projected
    normed = (summed * lax.rsqrt(lax.optimization_barrier(jnp.mean(summed * summed, axis=-1, keepdims=True)) + 1e-06) * norm_gain).astype(jnp.bfloat16)
    devices = N_SP * N_CP
    flat_ids = expert_ids.reshape(devices, TOK_DEV * TOP)
    one_hot = (flat_ids[:, :, None] == jnp.arange(EXPERTS, dtype=jnp.int32)[None, None, :]).astype(jnp.int32)
    before = jnp.cumsum(one_hot, axis=1, dtype=jnp.int32) - one_hot
    slot_rank = lax.optimization_barrier(jnp.sum(before * one_hot, axis=-1, dtype=jnp.int32))
    kept_mask = slot_rank < CAP
    slot_index = jnp.where(kept_mask, flat_ids * CAP + slot_rank, EXPERTS * CAP).astype(jnp.int32)
    device_rows = jnp.broadcast_to(jnp.arange(devices, dtype=jnp.int32)[:, None], slot_index.shape)
    owners = (jnp.arange(devices, dtype=jnp.int32)[:, None] * TOK_DEV + jnp.arange(TOK_DEV * TOP, dtype=jnp.int32)[None, :] // TOP).astype(jnp.int32)
    slot_table = jnp.full((devices, EXPERTS * CAP), -1, jnp.int32).at[device_rows, slot_index].set(owners, mode='drop')
    slot_weights = jnp.zeros((devices, EXPERTS * CAP), jnp.float32).at[device_rows, slot_index].set(route_weights.reshape(devices, TOK_DEV * TOP), mode='drop')
    slot_table = slot_table.reshape(devices, EXPERTS, CAP)
    slot_weights = slot_weights.reshape(devices, EXPERTS, CAP)
    part_width = FF_E // PARTS_SIZE

    def per_expert(moe_sum, expert_num):
        rows_idx = lax.dynamic_index_in_dim(slot_table, expert_num, 1, keepdims=False).reshape(-1)
        row_wts = lax.dynamic_index_in_dim(slot_weights, expert_num, 1, keepdims=False).reshape(-1)
        safe_rows = jnp.maximum(rows_idx, 0)
        picked = jnp.where((rows_idx >= 0)[:, None], normed[safe_rows], jnp.zeros((), jnp.bfloat16))
        total = jnp.zeros((devices * CAP, D), jnp.float32)
        for part_num in range(PARTS_SIZE):
            w_first = lax.dynamic_index_in_dim(expert_in, expert_num * PARTS_SIZE + part_num, 0, keepdims=False)
            w_second = lax.dynamic_index_in_dim(expert_out, expert_num * PARTS_SIZE + part_num, 0, keepdims=False)
            gate_up = jnp.dot(picked, w_first, preferred_element_type=jnp.float32)
            activated = (jax.nn.silu(gate_up[:, :part_width]) * gate_up[:, part_width:]).astype(jnp.bfloat16)
            part_out = jnp.dot(activated, w_second, preferred_element_type=jnp.float32).astype(jnp.bfloat16)
            total = total + part_out.astype(jnp.float32)
        expert_result = lax.optimization_barrier(total.astype(jnp.bfloat16)).astype(jnp.float32)
        moe_sum = moe_sum.at[safe_rows].add(row_wts[:, None] * expert_result)
        return (moe_sum, None)
    moe_sum, _ = lax.scan(per_expert, jnp.zeros((TOKENS, D), jnp.float32), jnp.arange(EXPERTS, dtype=jnp.int32))
    return (summed + moe_sum).astype(jnp.bfloat16)
```

```python
import math

import jax
import jax.numpy as jnp
from jax import lax
from jax.experimental import pallas as pl
from jax.experimental.pallas import tpu as pltpu
from jax.sharding import Mesh, PartitionSpec as P

NZ, NY, NX, NC = 8, 4, 4, 2
TOK = 128
HD = 128
KVH = 4
HEADS = 32
GROUP = HEADS // KVH
HG = 4
CAP = 8
DOC_MAX = 1024
SPAN = DOC_MAX + TOK
MESH_AXES = ("z", "y", "x", "c")
COUNT = NZ * NY * NX * NC
PLANE = NY * NX
BLOCK_ORDER = (0, 4, 1, 7, 2, 6, 3, 5)
MESH = pl.DeviceIdType.MESH


def place_of(block):
    sp, cp = block % (NZ * NY), block // (NZ * NY)
    return sp * NX * NC + cp


def from_behind(block, distance):
    route = [(place_of(i), place_of((i + distance) % COUNT)) for i in range(COUNT)]
    return lax.ppermute(block, MESH_AXES, route)


def attention_kernel(q_ref, kv_ref, bias_ref, out_ref, k_ref, v_ref):
    first = lax.axis_index("y")
    scale = math.log2(math.e) / math.sqrt(HD)
    for g in range(KVH):
        for b in range(SPAN // TOK):
            block = first + b
            rows = kv_ref[lax.rem(block, NY), block // NY]
            k_ref[b * TOK : (b + 1) * TOK, :] = rows[:, g * 2 * HD : g * 2 * HD + HD]
            v_ref[b * TOK : (b + 1) * TOK, :] = rows[:, g * 2 * HD + HD : (g + 1) * 2 * HD]

        for i in range(GROUP):
            head = g * GROUP + i
            q = q_ref[:, head * HD : (head + 1) * HD]
            scores = lax.dot_general(
                q, k_ref[...], (((1,), (1,)), ((), ())), preferred_element_type=jnp.float32
            )
            scores = scores * scale + bias_ref[...]
            top = jnp.max(scores, axis=-1, keepdims=True)
            exponent = jnp.exp2(scores - top)
            denominator = jnp.sum(exponent, axis=-1, keepdims=True)
            numerator = jnp.dot(
                exponent.astype(jnp.bfloat16), v_ref[...], preferred_element_type=jnp.float32
            )
            group, inner = head // HG, head % HG
            place = ((group % NC) * NX + group // NC) * HG + inner
            out_ref[:, place * HD : (place + 1) * HD] = (numerator / denominator).astype(
                jnp.bfloat16
            )


def attention(queries, kv_window, bias):
    return pl.pallas_call(
        attention_kernel,
        out_shape=jax.ShapeDtypeStruct(queries.shape, jnp.bfloat16),
        in_specs=[pl.BlockSpec(memory_space=pltpu.VMEM)] * 3,
        out_specs=pl.BlockSpec(memory_space=pltpu.VMEM),
        scratch_shapes=[
            pltpu.VMEM((SPAN, HD), jnp.bfloat16),
            pltpu.VMEM((SPAN, HD), jnp.bfloat16),
        ],
        compiler_params=pltpu.CompilerParams(vmem_limit_bytes=40 * 2**20),
        cost_estimate=pl.CostEstimate(
            flops=4 * HEADS * TOK * SPAN * HD, bytes_accessed=8 * 2**20, transcendentals=HEADS * TOK * SPAN
        ),
        name="attention",
    )(queries, kv_window, bias)


def moe_kernel(
    normed_ref,
    summed_ref,
    pick_ref,
    spread_ref,
    w_in_hbm,
    w_out_hbm,
    out_ref,
    col,
    stage,
    recv,
    result,
    back,
    acc,
    ring,
    home,
    w_in,
    w_out,
    own_sem,
    w_send,
    w_recv,
    col_send,
    col_recv,
    out_send,
    out_recv,
    back_send,
    back_recv,
    ring_send,
    ring_recv,
):
    z, y, x, c = (lax.axis_index(name) for name in MESH_AXES)
    right, left = lax.rem(z + 1, NZ), lax.rem(z + NZ - 1, NZ)
    place = y * NX + x
    model = normed_ref.shape[1]
    step = 512
    half = TOK // 2

    def peer(k):
        other_y, other_x = lax.rem(y + k // NX, NY), lax.rem(x + k % NX, NX)
        return {"y": other_y, "x": other_x}, other_y * NX + other_x

    barrier = pltpu.get_barrier_semaphore()

    def greet(k, carry):
        pl.semaphore_signal(barrier, inc=1, device_id=peer(k)[0], device_id_type=MESH)
        return carry

    lax.fori_loop(1, PLANE, greet, 0)
    for other in ({"z": right}, {"z": left}, {"c": 1 - c}):
        pl.semaphore_signal(barrier, inc=1, device_id=other, device_id_type=MESH)
    pl.semaphore_wait(barrier, PLANE - 1 + 3)

    def ring_copy(direction, number):
        source = number - 1 if direction == 0 else (NZ + 1 - number) % NZ
        target = number if direction == 0 else NZ - number
        rows = (0, TOK) if number < 4 else ((0, half) if direction == 0 else (half, half))

        def view(block):
            pair, side = (block, 0) if block < 4 else ((NZ - block) % 4, 1)
            return col.at[pair, pl.ds(side * TOK + rows[0], rows[1])]

        return pltpu.make_async_remote_copy(
            src_ref=view(source),
            dst_ref=view(target),
            send_sem=col_send.at[direction, number - 1],
            recv_sem=col_recv.at[direction, number - 1],
            device_id={"z": right if direction == 0 else left},
            device_id_type=MESH,
        )

    col[0, 0:TOK, :] = normed_ref[...]
    for direction in range(2):
        ring_copy(direction, 1).start()

    weight_copies = []
    for n, (hbm, vmem) in enumerate(((w_in_hbm, w_in), (w_out_hbm, w_out))):
        own = pltpu.make_async_copy(hbm.at[0], vmem.at[c], own_sem.at[n])
        given = pltpu.make_async_remote_copy(
            src_ref=hbm.at[0],
            dst_ref=vmem.at[c],
            send_sem=w_send.at[n],
            recv_sem=w_recv.at[n],
            device_id={"c": 1 - c},
            device_id_type=MESH,
        )
        own.start()
        given.start()
        weight_copies += [own, given]

    def exchange(source, target, sends, recvs, pair):
        def send(k, carry):
            device, expert = peer(k)
            pltpu.make_async_remote_copy(
                src_ref=source.at[pair, expert],
                dst_ref=target.at[pair, place],
                send_sem=sends.at[pair],
                recv_sem=recvs.at[pair],
                device_id=device,
                device_id_type=MESH,
            ).start()
            return carry

        lax.fori_loop(1, PLANE, send, 0)
        target[pair, place] = source[pair, place]

    def whole(source, target, sends, recvs, pair):
        return pltpu.make_async_remote_copy(
            src_ref=source.at[pair, pl.ds(0, PLANE - 1)],
            dst_ref=target.at[pair, pl.ds(0, PLANE - 1)],
            send_sem=sends.at[pair],
            recv_sem=recvs.at[pair],
            device_id={"y": y, "x": x},
            device_id_type=MESH,
        )

    for number in range(1, 5):
        pair = number % 4
        for direction in range(2):
            ring_copy(direction, number).wait_recv()
            if number < 4:
                ring_copy(direction, number + 1).start()

        def select(n, carry, pair=pair):
            columns = pl.ds(pl.multiple_of(n * step, step), step)
            rows = jnp.dot(
                pick_ref[pair], col[pair, :, columns], preferred_element_type=jnp.float32
            )
            stage[pair, :, :, columns] = rows.astype(jnp.bfloat16).reshape(PLANE, 2 * CAP, step)
            return carry

        lax.fori_loop(0, model // step, select, 0)
        exchange(stage, recv, out_send, out_recv, pair)

    for copy in weight_copies:
        copy.wait()

    def expert(pair):
        whole(stage, recv, out_send, out_recv, pair).wait_recv()
        rows = recv[pair].reshape(PLANE * 2 * CAP, model)
        width = w_out.shape[1]
        acts = []
        for p in range(2):
            gate_up = jnp.dot(rows, w_in[p], preferred_element_type=jnp.float32)
            gate, up = gate_up[:, :width], gate_up[:, width:]
            acts.append((gate / (1.0 + jnp.exp(-gate)) * up).astype(jnp.bfloat16))

        def down(n, carry):
            columns = pl.ds(pl.multiple_of(n * step, step), step)
            total = jnp.dot(acts[0], w_out[0, :, columns], preferred_element_type=jnp.float32)
            total += jnp.dot(acts[1], w_out[1, :, columns], preferred_element_type=jnp.float32)
            result[pair, :, :, columns] = total.astype(jnp.bfloat16).reshape(
                PLANE, 2 * CAP, step
            )
            return carry

        lax.fori_loop(0, model // step, down, 0)

    def early(n, carry):
        expert(n + 1)
        return carry

    lax.fori_loop(0, 3, early, 0)
    exchange(result, back, back_send, back_recv, 3)
    expert(0)
    for pair in (0, 2, 1):
        exchange(result, back, back_send, back_recv, pair)

    def sum_copy(direction, pair):
        if pair == 0:
            source = acc.at[0, pl.ds(TOK + direction * half, half)]
            target = ring.at[3, pl.ds(direction * (TOK + half), half)]
        else:
            source = acc.at[pair, pl.ds(direction * TOK, TOK)]
            target = ring.at[pair - 1, pl.ds(direction * TOK, TOK)]
        return pltpu.make_async_remote_copy(
            src_ref=source,
            dst_ref=target,
            send_sem=ring_send.at[direction, pair],
            recv_sem=ring_recv.at[direction, pair],
            device_id={"z": left if direction == 0 else right},
            device_id_type=MESH,
        )

    for pair in (0, 3, 2, 1):
        whole(result, back, back_send, back_recv, pair).wait_recv()
        if pair > 0:
            for direction in range(2):
                sum_copy(direction, (pair + 1) % 4).wait_recv()

        def weigh(n, carry, pair=pair):
            columns = pl.ds(pl.multiple_of(n * step, step), step)
            rows = back[pair, :, :, columns].reshape(PLANE * 2 * CAP, step)
            total = jnp.zeros((2 * TOK, step), jnp.float32)
            for part in range(2):
                total += lax.dot_general(
                    spread_ref[part, pair],
                    rows,
                    (((0,), (0,)), ((), ())),
                    preferred_element_type=jnp.float32,
                )
            if pair == 0:
                home[:, columns] = total[:TOK]
                acc[0, TOK:, columns] = total[TOK:].astype(jnp.bfloat16)
            elif pair == 3:
                low = ring[3, 0:half, columns].astype(jnp.float32)
                high = ring[3, TOK + half :, columns].astype(jnp.float32)
                acc[3, 0:half, columns] = (total[:half] + low).astype(jnp.bfloat16)
                acc[3, half : TOK + half, columns] = total[half : TOK + half].astype(jnp.bfloat16)
                acc[3, TOK + half :, columns] = (total[TOK + half :] + high).astype(jnp.bfloat16)
            else:
                came = ring[pair, :, columns].astype(jnp.float32)
                acc[pair, :, columns] = (total + came).astype(jnp.bfloat16)
            return carry

        lax.fori_loop(0, model // step, weigh, 0)
        for direction in range(2):
            sum_copy(direction, pair).start()

    for direction in range(2):
        sum_copy(direction, 1).wait_recv()

    def finish(n, carry):
        columns = pl.ds(pl.multiple_of(n * step, step), step)
        moe_sum = home[:, columns]
        moe_sum += ring[0, 0:TOK, columns].astype(jnp.float32)
        moe_sum += ring[0, TOK:, columns].astype(jnp.float32)
        out_ref[:, columns] = (summed_ref[:, columns] + moe_sum).astype(jnp.bfloat16)
        return carry

    lax.fori_loop(0, model // step, finish, 0)

    for pair in range(4):
        whole(stage, recv, out_send, out_recv, pair).wait_send()
        whole(result, back, back_send, back_recv, pair).wait_send()
        for direction in range(2):
            ring_copy(direction, pair + 1).wait_send()
            sum_copy(direction, pair).wait_send()


def moe(normed, summed, pick, spread, expert_in, expert_out):
    model = normed.shape[1]
    vmem, hbm = pl.BlockSpec(memory_space=pltpu.VMEM), pl.BlockSpec(memory_space=pl.ANY)
    slots = (4, PLANE, 2 * CAP, model)
    blocks = (4, 2 * TOK, model)
    dma = pltpu.SemaphoreType.DMA
    return pl.pallas_call(
        moe_kernel,
        out_shape=jax.ShapeDtypeStruct(normed.shape, jnp.bfloat16),
        in_specs=[vmem] * 4 + [hbm] * 2,
        out_specs=vmem,
        scratch_shapes=[
            pltpu.VMEM(blocks, jnp.bfloat16),
            pltpu.VMEM(slots, jnp.bfloat16),
            pltpu.VMEM(slots, jnp.bfloat16),
            pltpu.VMEM(slots, jnp.bfloat16),
            pltpu.VMEM(slots, jnp.bfloat16),
            pltpu.VMEM(blocks, jnp.bfloat16),
            pltpu.VMEM(blocks, jnp.bfloat16),
            pltpu.VMEM((TOK, model), jnp.float32),
            pltpu.VMEM((2,) + expert_in.shape[1:], jnp.bfloat16),
            pltpu.VMEM((2,) + expert_out.shape[1:], jnp.bfloat16),
            dma((2,)),
            dma((2,)),
            dma((2,)),
            dma((2, 4)),
            dma((2, 4)),
            dma((4,)),
            dma((4,)),
            dma((4,)),
            dma((4,)),
            dma((2, 4)),
            dma((2, 4)),
        ],
        compiler_params=pltpu.CompilerParams(
            collective_id=1, has_side_effects=True, vmem_limit_bytes=58 * 2**20
        ),
        cost_estimate=pl.CostEstimate(
            flops=10 * 10**9, bytes_accessed=12 * 2**20, transcendentals=0
        ),
        name="moe",
    )(normed, summed, pick, spread, expert_in, expert_out)


def on_device(
    queries,
    keyvals,
    residual,
    out_weight,
    norm_gain,
    doc_ids,
    expert_ids,
    route_weights,
    expert_in,
    expert_out,
):
    model = residual.shape[1]
    z, y = lax.axis_index("z"), lax.axis_index("y")
    number = ((lax.axis_index("x") * NC + lax.axis_index("c")) * NZ + z) * NY + y

    kv = keyvals.reshape(TOK, -1)
    back1 = from_behind(kv, NY)
    back2 = from_behind(back1, NY)
    kv_window = lax.all_gather(jnp.stack([back2, back1, kv]), "y")

    weight = lax.all_gather(out_weight, "x")
    weight = lax.all_gather(weight, "c").reshape(-1, model)

    routes = jnp.concatenate([expert_ids.astype(jnp.float32), route_weights], axis=1)
    routes = lax.all_gather(routes, "z")
    routes = jnp.take(routes, lax.rem(z + NZ - jnp.array(BLOCK_ORDER), NZ), axis=0)
    ids = routes[:, :, :8].astype(jnp.int32)
    plane_experts = z * PLANE + jnp.arange(PLANE, dtype=jnp.int32)
    hit = ids[:, :, :, None] == plane_experts
    chosen = jnp.any(hit, axis=2)
    weight_of = jnp.sum(jnp.where(hit, routes[:, :, 8:, None], 0.0), axis=2)
    earlier = jnp.tril(jnp.ones((TOK, TOK), jnp.bfloat16), -1)
    rank = jnp.einsum(
        "ts,bse->bte", earlier, chosen.astype(jnp.bfloat16), preferred_element_type=jnp.float32
    ).astype(jnp.int32)
    slot = jnp.where(chosen, rank, CAP)

    def by_expert(values):
        values = values.reshape(4, 2, TOK, PLANE).transpose(0, 3, 1, 2)
        return values.reshape(4, PLANE, 1, 1, 2 * TOK)

    row = jnp.arange(2 * CAP, dtype=jnp.int32)[:, None]
    side = jnp.arange(2 * TOK, dtype=jnp.int32)[None, :] // TOK
    taken = (by_expert(slot)[:, :, 0] == row % CAP) & (row // CAP == side)
    pick = taken.astype(jnp.bfloat16).reshape(4, 2 * TOK, 2 * TOK)
    spread = jnp.where(taken, by_expert(weight_of)[:, :, 0], 0.0).reshape(4, 2 * TOK, 2 * TOK)
    spread_high = lax.reduce_precision(spread, 8, 7)
    spread = jnp.stack([spread_high, spread - spread_high]).astype(jnp.bfloat16)

    padded = jnp.concatenate([jnp.full((DOC_MAX,), -1, jnp.int32), doc_ids], axis=0)
    key_docs = lax.dynamic_slice_in_dim(padded, number * TOK, SPAN, 0)
    query_docs = key_docs[DOC_MAX:]
    allowed = (key_docs[None, :] == query_docs[:, None]) & (
        jnp.arange(SPAN)[None, :] <= jnp.arange(TOK)[:, None] + DOC_MAX
    )
    bias = jnp.where(allowed, 0.0, -1e30).astype(jnp.float32)
    attended = attention(queries, kv_window, bias)

    summed = residual.astype(jnp.float32) + jnp.dot(
        attended, weight, preferred_element_type=jnp.float32
    )
    normed = (
        summed * lax.rsqrt(jnp.mean(summed * summed, axis=-1, keepdims=True) + 1e-06) * norm_gain
    ).astype(jnp.bfloat16)

    return moe(normed, summed, pick, spread, expert_in, expert_out)


def solution(mesh):
    torus = Mesh(mesh.devices.reshape(NZ, NY, NX, NC), ("z", "y", "x", "c"))
    tokens = ("x", "c", "z", "y")
    experts = ("z", "y", "x", "c")
    placed = (
        P(tokens, None),
        P(tokens, None, None),
        P(tokens, None),
        P(("x", "c"), None),
        P(),
        P(),
        P(tokens, None),
        P(tokens, None),
        P(experts, None, None),
        P(experts, None, None),
    )
    return jax.shard_map(
        on_device, mesh=torus, in_specs=placed, out_specs=P(tokens, None), check_vma=False
    )
```

```python
import math

import jax
import jax.numpy as jnp
from jax import lax
from jax.experimental import pallas as pl
from jax.experimental.pallas import tpu as pltpu
from jax.sharding import Mesh, PartitionSpec as P

NZ, NY, NX, NC = 8, 4, 4, 2
TOK = 128
HD = 128
KVH = 4
HEADS = 32
GROUP = HEADS // KVH
HG = 4
CAP = 8
DOC_MAX = 1024
SPAN = DOC_MAX + TOK
MESH_AXES = ("z", "y", "x", "c")
COUNT = NZ * NY * NX * NC
PLANE = NY * NX
BLOCK_ORDER = (0, 4, 1, 7, 2, 6, 3, 5)
MESH = pl.DeviceIdType.MESH


def front_kernel(
    q_ref,
    kv_ref,
    bias_ref,
    routes_ref,
    residual_ref,
    gain_ref,
    weight_hbm,
    summed_ref,
    normed_ref,
    routes_out,
    window,
    attended,
    arrived,
    weight,
    share,
    shares_in,
    own,
    routes_in,
    own_sem,
    w_send,
    w_recv,
    route_send,
    route_recv,
    z_send,
    z_recv,
    y_send,
    y_recv,
    att_send,
    att_recv,
    share_send,
    share_recv,
):
    z, y, x, c = (lax.axis_index(name) for name in MESH_AXES)
    model = residual_ref.shape[1]
    scale = math.log2(math.e) / math.sqrt(HD)

    cp = x * NC + c
    wrap = (z + 1) // NZ
    cp_ahead = lax.rem(cp + wrap, NX * NC)
    ahead = {"z": lax.rem(z + 1, NZ), "x": cp_ahead // NC, "c": lax.rem(cp_ahead, NC)}
    wrap = 1 - (z + NZ - 1) // NZ
    cp_behind = lax.rem(cp + NX * NC - wrap, NX * NC)
    behind = {
        "z": lax.rem(z + NZ - 1, NZ),
        "x": cp_behind // NC,
        "c": lax.rem(cp_behind, NC),
    }

    def along(axis, position, distance, size):
        return {axis: lax.rem(position + distance, size)}

    barrier = pltpu.get_barrier_semaphore()
    others = [ahead, behind, {"c": 1 - c}]
    others += [along("y", y, d, NY) for d in range(1, NY)]
    others += [along("x", x, d, NX) for d in range(1, NX)]
    others += [along("z", z, d, NZ) for d in range(1, NZ)]
    for other in others:
        pl.semaphore_signal(barrier, inc=1, device_id=other, device_id_type=MESH)
    pl.semaphore_wait(barrier, len(others))

    def remote(source, target, send, recv, device):
        return pltpu.make_async_remote_copy(
            src_ref=source,
            dst_ref=target,
            send_sem=send,
            recv_sem=recv,
            device_id=device,
            device_id_type=MESH,
        )

    def hop(g, number):
        source = window.at[g, (3 - number) * NY + y]
        target = window.at[g, (2 - number) * NY + y]
        return remote(
            source, target, z_send.at[g, number - 1], z_recv.at[g, number - 1], ahead
        )

    def to_row(g, plane, d):
        block = window.at[g, plane * NY + y]
        return remote(
            block,
            block,
            y_send.at[g, plane, d - 1],
            y_recv.at[g, plane, d - 1],
            along("y", y, d, NY),
        )

    def route_copy(d):
        return remote(
            routes_ref,
            routes_in.at[BLOCK_ORDER.index(d)],
            route_send.at[d],
            route_recv.at[d],
            along("z", z, d, NZ),
        )

    def rotated(n):
        return lax.rem(x + 1 + n, KVH)

    def first(n, carry):
        g = rotated(n)
        window[g, 2 * NY + y] = kv_ref[g]
        hop(g, 1).start()
        for d in range(1, NY):

            @pl.when(y + d < NY)
            def _():
                to_row(g, 2, d).start()

        return carry

    lax.fori_loop(0, KVH, first, 0)

    own_weight = pltpu.make_async_copy(weight_hbm, weight.at[c], own_sem)
    own_weight.start()
    given_weight = remote(weight_hbm, weight.at[c], w_send, w_recv, {"c": 1 - c})
    given_weight.start()
    for d in range(1, NZ):
        route_copy(d).start()

    def second(n, carry):
        g = rotated(n)
        hop(g, 1).wait_recv()
        hop(g, 2).start()
        for d in range(1, NY):
            to_row(g, 1, d).start()
        return carry

    lax.fori_loop(0, KVH, second, 0)

    def third(n, carry):
        g = rotated(n)
        hop(g, 2).wait_recv()
        for d in range(1, NY):

            @pl.when(y + d >= NY)
            def _():
                to_row(g, 0, d).start()

        return carry

    lax.fori_loop(0, KVH, third, 0)

    own_weight.wait()
    given_weight.wait()

    def attend_copy(n):
        g = rotated(n)
        return remote(
            attended.at[g], arrived.at[x], att_send.at[n], att_recv.at[n], {"x": g}
        )

    def source_of(n):
        return lax.rem(x + NX - 1 - n, NX)

    def share_copy(n):
        source = source_of(n)
        return remote(
            share.at[n], shares_in.at[n], share_send.at[n], share_recv.at[n], {"x": source}
        )

    step = 512

    def product(rows, columns):
        total = jnp.dot(rows[:, : HG * HD], weight[0, :, columns], preferred_element_type=jnp.float32)
        total += jnp.dot(rows[:, HG * HD :], weight[1, :, columns], preferred_element_type=jnp.float32)
        return total

    def project(n):
        attend_copy(n).wait_recv()
        rows = arrived[source_of(n)]

        def part(m, carry):
            columns = pl.ds(pl.multiple_of(m * step, step), step)
            share[n, :, columns] = product(rows, columns).astype(jnp.bfloat16)
            return carry

        lax.fori_loop(0, model // step, part, 0)
        share_copy(n).start()

    def one_kv_head(n, carry):
        g = rotated(n)
        for d in range(1, NY):
            to_row(g, 1, d).wait_recv()

            @pl.when(y >= d)
            def _():
                to_row(g, 2, d).wait_recv()

            @pl.when(y < d)
            def _():
                to_row(g, 0, d).wait_recv()

        keys = window[g, pl.ds(y, SPAN // TOK), :, 0:HD].reshape(SPAN, HD)
        values = window[g, pl.ds(y, SPAN // TOK), :, HD:].reshape(SPAN, HD)
        for i in range(GROUP):
            q = q_ref[:, pl.ds(pl.multiple_of(g * GROUP * HD + i * HD, HD), HD)]
            scores = lax.dot_general(
                q, keys, (((1,), (1,)), ((), ())), preferred_element_type=jnp.float32
            )
            scores = scores * scale + bias_ref[...]
            top = jnp.max(scores, axis=-1, keepdims=True)
            exponent = jnp.exp2(scores - top)
            denominator = jnp.sum(exponent, axis=-1, keepdims=True)
            numerator = jnp.dot(
                exponent.astype(jnp.bfloat16), values, preferred_element_type=jnp.float32
            )
            attended[g, :, i * HD : (i + 1) * HD] = (numerator / denominator).astype(jnp.bfloat16)

        @pl.when(n < NX - 1)
        def _():
            attend_copy(n).start()

        @pl.when(n > 0)
        def _():
            project(n - 1)

        return carry

    lax.fori_loop(0, KVH, one_kv_head, 0)

    mine = attended[x]

    def own_part(m, carry):
        columns = pl.ds(pl.multiple_of(m * step, step), step)
        own[:, columns] = product(mine, columns)
        return carry

    lax.fori_loop(0, model // step, own_part, 0)

    for n in range(NX - 1):
        share_copy(n).wait_recv()

    def finish(m, carry):
        rows = pl.ds(pl.multiple_of(m * 32, 32), 32)
        summed = residual_ref[rows].astype(jnp.float32) + own[rows]
        for n in range(NX - 1):
            summed += shares_in[n, rows].astype(jnp.float32)
        summed_ref[rows] = summed
        mean = jnp.mean(summed * summed, axis=-1, keepdims=True)
        normed_ref[rows] = (summed * lax.rsqrt(mean + 1e-06) * gain_ref[...]).astype(jnp.bfloat16)
        return carry

    lax.fori_loop(0, TOK // 32, finish, 0)

    routes_in[0] = routes_ref[...]
    for d in range(1, NZ):
        route_copy(d).wait()
    routes_out[...] = routes_in[...]

    def drain(g, carry):
        for number in (1, 2):
            hop(g, number).wait_send()
        for d in range(1, NY):
            to_row(g, 1, d).wait_send()

            @pl.when(y + d < NY)
            def _():
                to_row(g, 2, d).wait_send()

            @pl.when(y + d >= NY)
            def _():
                to_row(g, 0, d).wait_send()

        return carry

    lax.fori_loop(0, KVH, drain, 0)
    for n in range(NX - 1):
        attend_copy(n).wait_send()
        share_copy(n).wait_send()


def front(queries, keyvals, bias, routes, residual, gain, out_weight):
    model = residual.shape[1]
    vmem, hbm = pl.BlockSpec(memory_space=pltpu.VMEM), pl.BlockSpec(memory_space=pl.ANY)
    dma = pltpu.SemaphoreType.DMA
    half = HEADS * HD // NX
    bf16, f32 = jnp.bfloat16, jnp.float32
    return pl.pallas_call(
        front_kernel,
        out_shape=(
            jax.ShapeDtypeStruct((TOK, model), f32),
            jax.ShapeDtypeStruct((TOK, model), bf16),
            jax.ShapeDtypeStruct((NZ,) + routes.shape, f32),
        ),
        in_specs=[vmem] * 6 + [hbm],
        out_specs=(vmem,) * 3,
        scratch_shapes=[
            pltpu.VMEM((KVH, 3 * NY, TOK, 2 * HD), bf16),
            pltpu.VMEM((KVH, TOK, half), bf16),
            pltpu.VMEM((NX, TOK, half), bf16),
            pltpu.VMEM((NC,) + out_weight.shape, bf16),
            pltpu.VMEM((NX - 1, TOK, model), bf16),
            pltpu.VMEM((NX - 1, TOK, model), bf16),
            pltpu.VMEM((TOK, model), f32),
            pltpu.VMEM((NZ,) + routes.shape, f32),
            dma,
            dma,
            dma,
            dma((NZ,)),
            dma((NZ,)),
            dma((KVH, 2)),
            dma((KVH, 2)),
            dma((KVH, 3, NY - 1)),
            dma((KVH, 3, NY - 1)),
            dma((NX - 1,)),
            dma((NX - 1,)),
            dma((NX - 1,)),
            dma((NX - 1,)),
        ],
        compiler_params=pltpu.CompilerParams(
            collective_id=2, has_side_effects=True, vmem_limit_bytes=48 * 2**20
        ),
        cost_estimate=pl.CostEstimate(
            flops=4 * 10**9, bytes_accessed=8 * 2**20, transcendentals=HEADS * TOK * SPAN
        ),
        name="front",
    )(queries, keyvals, bias, routes, residual, gain, out_weight)


def moe_kernel(
    normed_ref,
    summed_ref,
    pick_ref,
    spread_ref,
    w_in_hbm,
    w_out_hbm,
    out_ref,
    col,
    stage,
    recv,
    result,
    back,
    acc,
    ring,
    home,
    w_in,
    w_out,
    own_sem,
    w_send,
    w_recv,
    col_send,
    col_recv,
    out_send,
    out_recv,
    back_send,
    back_recv,
    ring_send,
    ring_recv,
):
    z, y, x, c = (lax.axis_index(name) for name in MESH_AXES)
    right, left = lax.rem(z + 1, NZ), lax.rem(z + NZ - 1, NZ)
    place = y * NX + x
    model = normed_ref.shape[1]
    step = 512
    half = TOK // 2

    def peer(k):
        other_y, other_x = lax.rem(y + k // NX, NY), lax.rem(x + k % NX, NX)
        return {"y": other_y, "x": other_x}, other_y * NX + other_x

    barrier = pltpu.get_barrier_semaphore()

    def greet(k, carry):
        pl.semaphore_signal(barrier, inc=1, device_id=peer(k)[0], device_id_type=MESH)
        return carry

    lax.fori_loop(1, PLANE, greet, 0)
    for other in ({"z": right}, {"z": left}, {"c": 1 - c}):
        pl.semaphore_signal(barrier, inc=1, device_id=other, device_id_type=MESH)
    pl.semaphore_wait(barrier, PLANE - 1 + 3)

    def ring_copy(direction, number):
        source = number - 1 if direction == 0 else (NZ + 1 - number) % NZ
        target = number if direction == 0 else NZ - number
        rows = (0, TOK) if number < 4 else ((0, half) if direction == 0 else (half, half))

        def view(block):
            pair, side = (block, 0) if block < 4 else ((NZ - block) % 4, 1)
            return col.at[pair, pl.ds(side * TOK + rows[0], rows[1])]

        return pltpu.make_async_remote_copy(
            src_ref=view(source),
            dst_ref=view(target),
            send_sem=col_send.at[direction, number - 1],
            recv_sem=col_recv.at[direction, number - 1],
            device_id={"z": right if direction == 0 else left},
            device_id_type=MESH,
        )

    col[0, 0:TOK, :] = normed_ref[...]
    for direction in range(2):
        ring_copy(direction, 1).start()

    weight_copies = []
    for n, (hbm, vmem) in enumerate(((w_in_hbm, w_in), (w_out_hbm, w_out))):
        own = pltpu.make_async_copy(hbm.at[0], vmem.at[c], own_sem.at[n])
        given = pltpu.make_async_remote_copy(
            src_ref=hbm.at[0],
            dst_ref=vmem.at[c],
            send_sem=w_send.at[n],
            recv_sem=w_recv.at[n],
            device_id={"c": 1 - c},
            device_id_type=MESH,
        )
        own.start()
        given.start()
        weight_copies += [own, given]

    def exchange(source, target, sends, recvs, pair):
        def send(k, carry):
            device, expert = peer(k)
            pltpu.make_async_remote_copy(
                src_ref=source.at[pair, expert],
                dst_ref=target.at[pair, place],
                send_sem=sends.at[pair],
                recv_sem=recvs.at[pair],
                device_id=device,
                device_id_type=MESH,
            ).start()
            return carry

        lax.fori_loop(1, PLANE, send, 0)
        target[pair, place] = source[pair, place]

    def whole(source, target, sends, recvs, pair):
        return pltpu.make_async_remote_copy(
            src_ref=source.at[pair, pl.ds(0, PLANE - 1)],
            dst_ref=target.at[pair, pl.ds(0, PLANE - 1)],
            send_sem=sends.at[pair],
            recv_sem=recvs.at[pair],
            device_id={"y": y, "x": x},
            device_id_type=MESH,
        )

    for number in range(1, 5):
        pair = number % 4
        for direction in range(2):
            ring_copy(direction, number).wait_recv()
            if number < 4:
                ring_copy(direction, number + 1).start()

        def select(n, carry, pair=pair):
            columns = pl.ds(pl.multiple_of(n * step, step), step)
            rows = jnp.dot(
                pick_ref[pair], col[pair, :, columns], preferred_element_type=jnp.float32
            )
            stage[pair, :, :, columns] = rows.astype(jnp.bfloat16).reshape(PLANE, 2 * CAP, step)
            return carry

        lax.fori_loop(0, model // step, select, 0)
        exchange(stage, recv, out_send, out_recv, pair)

    for copy in weight_copies:
        copy.wait()

    def expert(pair):
        whole(stage, recv, out_send, out_recv, pair).wait_recv()
        rows = recv[pair].reshape(PLANE * 2 * CAP, model)
        width = w_out.shape[1]
        acts = []
        for p in range(2):
            gate_up = jnp.dot(rows, w_in[p], preferred_element_type=jnp.float32)
            gate, up = gate_up[:, :width], gate_up[:, width:]
            acts.append((gate / (1.0 + jnp.exp(-gate)) * up).astype(jnp.bfloat16))

        def down(n, carry):
            columns = pl.ds(pl.multiple_of(n * step, step), step)
            total = jnp.dot(acts[0], w_out[0, :, columns], preferred_element_type=jnp.float32)
            total += jnp.dot(acts[1], w_out[1, :, columns], preferred_element_type=jnp.float32)
            result[pair, :, :, columns] = total.astype(jnp.bfloat16).reshape(
                PLANE, 2 * CAP, step
            )
            return carry

        lax.fori_loop(0, model // step, down, 0)

    def early(n, carry):
        expert(n + 1)
        return carry

    lax.fori_loop(0, 3, early, 0)
    exchange(result, back, back_send, back_recv, 3)
    expert(0)
    for pair in (0, 2, 1):
        exchange(result, back, back_send, back_recv, pair)

    def sum_copy(direction, pair):
        if pair == 0:
            source = acc.at[0, pl.ds(TOK + direction * half, half)]
            target = ring.at[3, pl.ds(direction * (TOK + half), half)]
        else:
            source = acc.at[pair, pl.ds(direction * TOK, TOK)]
            target = ring.at[pair - 1, pl.ds(direction * TOK, TOK)]
        return pltpu.make_async_remote_copy(
            src_ref=source,
            dst_ref=target,
            send_sem=ring_send.at[direction, pair],
            recv_sem=ring_recv.at[direction, pair],
            device_id={"z": left if direction == 0 else right},
            device_id_type=MESH,
        )

    for pair in (0, 3, 2, 1):
        whole(result, back, back_send, back_recv, pair).wait_recv()
        if pair > 0:
            for direction in range(2):
                sum_copy(direction, (pair + 1) % 4).wait_recv()

        def weigh(n, carry, pair=pair):
            columns = pl.ds(pl.multiple_of(n * step, step), step)
            rows = back[pair, :, :, columns].reshape(PLANE * 2 * CAP, step)
            total = jnp.zeros((2 * TOK, step), jnp.float32)
            for part in range(2):
                total += lax.dot_general(
                    spread_ref[part, pair],
                    rows,
                    (((0,), (0,)), ((), ())),
                    preferred_element_type=jnp.float32,
                )
            if pair == 0:
                home[:, columns] = total[:TOK]
                acc[0, TOK:, columns] = total[TOK:].astype(jnp.bfloat16)
            elif pair == 3:
                low = ring[3, 0:half, columns].astype(jnp.float32)
                high = ring[3, TOK + half :, columns].astype(jnp.float32)
                acc[3, 0:half, columns] = (total[:half] + low).astype(jnp.bfloat16)
                acc[3, half : TOK + half, columns] = total[half : TOK + half].astype(jnp.bfloat16)
                acc[3, TOK + half :, columns] = (total[TOK + half :] + high).astype(jnp.bfloat16)
            else:
                came = ring[pair, :, columns].astype(jnp.float32)
                acc[pair, :, columns] = (total + came).astype(jnp.bfloat16)
            return carry

        lax.fori_loop(0, model // step, weigh, 0)
        for direction in range(2):
            sum_copy(direction, pair).start()

    for direction in range(2):
        sum_copy(direction, 1).wait_recv()

    def finish(n, carry):
        columns = pl.ds(pl.multiple_of(n * step, step), step)
        moe_sum = home[:, columns]
        moe_sum += ring[0, 0:TOK, columns].astype(jnp.float32)
        moe_sum += ring[0, TOK:, columns].astype(jnp.float32)
        out_ref[:, columns] = (summed_ref[:, columns] + moe_sum).astype(jnp.bfloat16)
        return carry

    lax.fori_loop(0, model // step, finish, 0)

    for pair in range(4):
        whole(stage, recv, out_send, out_recv, pair).wait_send()
        whole(result, back, back_send, back_recv, pair).wait_send()
        for direction in range(2):
            ring_copy(direction, pair + 1).wait_send()
            sum_copy(direction, pair).wait_send()


def moe(normed, summed, pick, spread, expert_in, expert_out):
    model = normed.shape[1]
    vmem, hbm = pl.BlockSpec(memory_space=pltpu.VMEM), pl.BlockSpec(memory_space=pl.ANY)
    slots = (4, PLANE, 2 * CAP, model)
    blocks = (4, 2 * TOK, model)
    dma = pltpu.SemaphoreType.DMA
    return pl.pallas_call(
        moe_kernel,
        out_shape=jax.ShapeDtypeStruct(normed.shape, jnp.bfloat16),
        in_specs=[vmem] * 4 + [hbm] * 2,
        out_specs=vmem,
        scratch_shapes=[
            pltpu.VMEM(blocks, jnp.bfloat16),
            pltpu.VMEM(slots, jnp.bfloat16),
            pltpu.VMEM(slots, jnp.bfloat16),
            pltpu.VMEM(slots, jnp.bfloat16),
            pltpu.VMEM(slots, jnp.bfloat16),
            pltpu.VMEM(blocks, jnp.bfloat16),
            pltpu.VMEM(blocks, jnp.bfloat16),
            pltpu.VMEM((TOK, model), jnp.float32),
            pltpu.VMEM((2,) + expert_in.shape[1:], jnp.bfloat16),
            pltpu.VMEM((2,) + expert_out.shape[1:], jnp.bfloat16),
            dma((2,)),
            dma((2,)),
            dma((2,)),
            dma((2, 4)),
            dma((2, 4)),
            dma((4,)),
            dma((4,)),
            dma((4,)),
            dma((4,)),
            dma((2, 4)),
            dma((2, 4)),
        ],
        compiler_params=pltpu.CompilerParams(
            collective_id=1, has_side_effects=True, vmem_limit_bytes=58 * 2**20
        ),
        cost_estimate=pl.CostEstimate(
            flops=10 * 10**9, bytes_accessed=12 * 2**20, transcendentals=0
        ),
        name="moe",
    )(normed, summed, pick, spread, expert_in, expert_out)


def on_device(
    queries,
    keyvals,
    residual,
    out_weight,
    norm_gain,
    doc_ids,
    expert_ids,
    route_weights,
    expert_in,
    expert_out,
):
    model = residual.shape[1]
    z, y = lax.axis_index("z"), lax.axis_index("y")
    number = ((lax.axis_index("x") * NC + lax.axis_index("c")) * NZ + z) * NY + y

    padded = jnp.concatenate([jnp.full((DOC_MAX,), -1, jnp.int32), doc_ids], axis=0)
    key_docs = lax.dynamic_slice_in_dim(padded, number * TOK, SPAN, 0)
    query_docs = key_docs[DOC_MAX:]
    allowed = (key_docs[None, :] == query_docs[:, None]) & (
        jnp.arange(SPAN)[None, :] <= jnp.arange(TOK)[:, None] + DOC_MAX
    )
    bias = jnp.where(allowed, 0.0, -1e30).astype(jnp.float32)
    routes = jnp.concatenate([expert_ids.astype(jnp.float32), route_weights], axis=1)
    summed, normed, routes = front(
        queries, keyvals.transpose(1, 0, 2), bias, routes.T, residual, norm_gain[None], out_weight
    )

    ids = routes[:, :8].astype(jnp.int32)
    plane_experts = z * PLANE + jnp.arange(PLANE, dtype=jnp.int32)
    hit = ids[:, None] == plane_experts[:, None, None]
    chosen = jnp.any(hit, axis=2)
    weight_of = jnp.sum(jnp.where(hit, routes[:, None, 8:], 0.0), axis=2)
    earlier = jnp.triu(jnp.ones((TOK, TOK), jnp.bfloat16), 1)
    rank = jnp.einsum(
        "bes,st->bet", chosen.astype(jnp.bfloat16), earlier, preferred_element_type=jnp.float32
    ).astype(jnp.int32)
    slot = jnp.where(chosen, rank, CAP)

    def by_expert(values):
        values = values.reshape(4, 2, PLANE, TOK).transpose(0, 2, 1, 3)
        return values.reshape(4, PLANE, 1, 1, 2 * TOK)

    row = jnp.arange(2 * CAP, dtype=jnp.int32)[:, None]
    side = jnp.arange(2 * TOK, dtype=jnp.int32)[None, :] // TOK
    taken = (by_expert(slot)[:, :, 0] == row % CAP) & (row // CAP == side)
    pick = taken.astype(jnp.bfloat16).reshape(4, 2 * TOK, 2 * TOK)
    spread = jnp.where(taken, by_expert(weight_of)[:, :, 0], 0.0).reshape(4, 2 * TOK, 2 * TOK)
    spread_high = lax.reduce_precision(spread, 8, 7)
    spread = jnp.stack([spread_high, spread - spread_high]).astype(jnp.bfloat16)

    return moe(normed, summed, pick, spread, expert_in, expert_out)


def solution(mesh):
    torus = Mesh(mesh.devices.reshape(NZ, NY, NX, NC), ("z", "y", "x", "c"))
    tokens = ("x", "c", "z", "y")
    experts = ("z", "y", "x", "c")
    placed = (
        P(tokens, None),
        P(tokens, None, None),
        P(tokens, None),
        P(("x", "c"), None),
        P(),
        P(),
        P(tokens, None),
        P(tokens, None),
        P(experts, None, None),
        P(experts, None, None),
    )
    return jax.shard_map(
        on_device, mesh=torus, in_specs=placed, out_specs=P(tokens, None), check_vma=False
    )
```

```python
import math

import jax
import jax.numpy as jnp
from jax import lax
from jax.experimental import pallas as pl
from jax.experimental.pallas import tpu as pltpu
from jax.sharding import Mesh, PartitionSpec as P

NZ, NY, NX, NC = 8, 4, 4, 2
TOK = 128
HD = 128
KVH = 4
HEADS = 32
GROUP = HEADS // KVH
HG = 4
CAP = 8
DOC_MAX = 1024
SPAN = DOC_MAX + TOK
MESH_AXES = ("z", "y", "x", "c")
COUNT = NZ * NY * NX * NC
PLANE = NY * NX
MESH = pl.DeviceIdType.MESH


def layer_kernel(
    queries_hbm,
    kv_ref,
    key_docs_ref,
    query_docs_ref,
    routes_ref,
    residual_hbm,
    gain_ref,
    weight_hbm,
    w_in_hbm,
    w_out_hbm,
    out_ref,
    queries,
    residual,
    bias,
    window,
    attended,
    arrived,
    weight,
    share,
    shares_in,
    own,
    routes_in,
    col,
    stage,
    recv,
    back,
    acc,
    ring,
    home,
    slot_of,
    weight_of,
    w_in,
    w_out,
    load_sem,
    given_send,
    given_recv,
    route_send,
    route_recv,
    z_send,
    z_recv,
    y_send,
    y_recv,
    att_send,
    att_recv,
    share_send,
    share_recv,
    own_sem,
    w_send,
    w_recv,
    col_send,
    col_recv,
    out_send,
    out_recv,
    back_send,
    back_recv,
    ring_send,
    ring_recv,
):
    z, y, x, c = (lax.axis_index(name) for name in MESH_AXES)
    model = residual.shape[1]
    wide = model // 2
    scale = math.log2(math.e) / math.sqrt(HD)

    cp = x * NC + c
    wrap = (z + 1) // NZ
    cp_ahead = lax.rem(cp + wrap, NX * NC)
    ahead = {"z": lax.rem(z + 1, NZ), "x": cp_ahead // NC, "c": lax.rem(cp_ahead, NC)}
    wrap = 1 - (z + NZ - 1) // NZ
    cp_behind = lax.rem(cp + NX * NC - wrap, NX * NC)
    behind = {
        "z": lax.rem(z + NZ - 1, NZ),
        "x": cp_behind // NC,
        "c": lax.rem(cp_behind, NC),
    }

    def along(axis, position, distance, size):
        return {axis: lax.rem(position + distance, size)}

    def peer(k):
        other_y, other_x = lax.rem(y + k // NX, NY), lax.rem(x + k % NX, NX)
        return {"y": other_y, "x": other_x}, other_y * NX + other_x

    barrier = pltpu.get_barrier_semaphore()

    def greet(k, carry):
        pl.semaphore_signal(barrier, inc=1, device_id=peer(k)[0], device_id_type=MESH)
        return carry

    lax.fori_loop(1, PLANE, greet, 0)
    others = [ahead, behind, {"c": 1 - c}]
    others += [along("z", z, d, NZ) for d in range(1, NZ)]
    for other in others:
        pl.semaphore_signal(barrier, inc=1, device_id=other, device_id_type=MESH)
    pl.semaphore_wait(barrier, PLANE - 1 + len(others))

    def remote(source, target, send, recv, device):
        return pltpu.make_async_remote_copy(
            src_ref=source,
            dst_ref=target,
            send_sem=send,
            recv_sem=recv,
            device_id=device,
            device_id_type=MESH,
        )

    def hop(g, number):
        source = window.at[g, (3 - number) * NY + y]
        target = window.at[g, (2 - number) * NY + y]
        return remote(
            source, target, z_send.at[g, number - 1], z_recv.at[g, number - 1], ahead
        )

    def to_row(g, plane, d):
        block = window.at[g, plane * NY + y]
        return remote(
            block,
            block,
            y_send.at[g, plane, d - 1],
            y_recv.at[g, plane, d - 1],
            along("y", y, d, NY),
        )

    def route_copy(d):
        return remote(
            routes_ref,
            routes_in.at[d],
            route_send.at[d],
            route_recv.at[d],
            along("z", z, d, NZ),
        )

    def rotated(n):
        return lax.rem(x + 1 + n, KVH)

    def first(n, carry):
        g = rotated(n)
        window[g, 2 * NY + y] = kv_ref[g]
        hop(g, 1).start()
        for d in range(1, NY):

            @pl.when(y + d < NY)
            def _():
                to_row(g, 2, d).start()

        return carry

    lax.fori_loop(0, KVH, first, 0)

    for d in range(1, NZ):
        route_copy(d).start()
    loads = [
        pltpu.make_async_copy(queries_hbm, queries, load_sem.at[0]),
        pltpu.make_async_copy(residual_hbm, residual, load_sem.at[1]),
        pltpu.make_async_copy(weight_hbm, weight.at[c], load_sem.at[2]),
        remote(weight_hbm, weight.at[c], given_send, given_recv, {"c": 1 - c}),
    ]
    for load in loads:
        load.start()

    def second(n, carry):
        g = rotated(n)
        hop(g, 1).wait_recv()
        hop(g, 2).start()
        for d in range(1, NY):
            to_row(g, 1, d).start()
        return carry

    lax.fori_loop(0, KVH, second, 0)

    keys_at = lax.broadcasted_iota(jnp.int32, (TOK, SPAN), 1)
    tokens_at = lax.broadcasted_iota(jnp.int32, (TOK, SPAN), 0) + DOC_MAX
    allowed = (key_docs_ref[...] == query_docs_ref[...]) & (keys_at <= tokens_at)
    bias[...] = jnp.where(allowed, 0.0, -1e30)

    def third(n, carry):
        g = rotated(n)
        hop(g, 2).wait_recv()
        for d in range(1, NY):

            @pl.when(y + d >= NY)
            def _():
                to_row(g, 0, d).start()

        return carry

    lax.fori_loop(0, KVH, third, 0)

    weight_copies = []
    for n, (hbm, vmem) in enumerate(((w_in_hbm, w_in), (w_out_hbm, w_out))):
        own_part = pltpu.make_async_copy(hbm.at[0], vmem.at[c], own_sem.at[n])
        given = remote(hbm.at[0], vmem.at[c], w_send.at[n], w_recv.at[n], {"c": 1 - c})
        own_part.start()
        given.start()
        weight_copies += [own_part, given]

    for load in loads:
        load.wait()

    def attend_copy(n):
        g = rotated(n)
        return remote(
            attended.at[g], arrived.at[x], att_send.at[n], att_recv.at[n], {"x": g}
        )

    def source_of(n):
        return lax.rem(x + NX - 1 - n, NX)

    def share_copy(n):
        source = source_of(n)
        return remote(
            share.at[n], shares_in.at[n], share_send.at[n], share_recv.at[n], {"x": source}
        )

    step = 512

    def product(rows, columns):
        total = jnp.dot(rows[:, : HG * HD], weight[0, :, columns], preferred_element_type=jnp.float32)
        total += jnp.dot(rows[:, HG * HD :], weight[1, :, columns], preferred_element_type=jnp.float32)
        return total

    def project(n):
        attend_copy(n).wait_recv()
        rows = arrived[source_of(n)]

        def part(m, carry):
            columns = pl.ds(pl.multiple_of(m * step, step), step)
            share[n, :, columns] = product(rows, columns).astype(jnp.bfloat16)
            return carry

        lax.fori_loop(0, model // step, part, 0)
        share_copy(n).start()

    def one_kv_head(n, carry):
        g = rotated(n)
        for d in range(1, NY):
            to_row(g, 1, d).wait_recv()

            @pl.when(y >= d)
            def _():
                to_row(g, 2, d).wait_recv()

            @pl.when(y < d)
            def _():
                to_row(g, 0, d).wait_recv()

        keys = window[g, pl.ds(y, SPAN // TOK), :, 0:HD].reshape(SPAN, HD)
        values = window[g, pl.ds(y, SPAN // TOK), :, HD:].reshape(SPAN, HD)
        for i in range(0, GROUP, 2):
            first_column = g * GROUP * HD + i * HD
            q = [
                queries[:, pl.ds(pl.multiple_of(first_column + k * HD, HD), HD)] for k in range(2)
            ]
            scores = lax.dot_general(
                jnp.concatenate(q, axis=0),
                keys,
                (((1,), (1,)), ((), ())),
                preferred_element_type=jnp.float32,
            )
            scores = scores.reshape(2, TOK, SPAN) * scale + bias[...]
            top = jnp.max(scores, axis=-1, keepdims=True)
            exponent = jnp.exp2(scores - top)
            denominator = jnp.sum(exponent, axis=-1, keepdims=True)
            numerator = jnp.dot(
                exponent.astype(jnp.bfloat16).reshape(2 * TOK, SPAN),
                values,
                preferred_element_type=jnp.float32,
            )
            result = (numerator.reshape(2, TOK, HD) / denominator).astype(jnp.bfloat16)
            for k in range(2):
                attended[g, :, (i + k) * HD : (i + k + 1) * HD] = result[k]

        @pl.when(n < NX - 1)
        def _():
            attend_copy(n).start()

        @pl.when(n > 0)
        def _():
            project(n - 1)

        return carry

    lax.fori_loop(0, KVH, one_kv_head, 0)

    mine = attended[x]

    def own_product(m, carry):
        columns = pl.ds(pl.multiple_of(m * step, step), step)
        own[:, columns] = product(mine, columns)
        return carry

    lax.fori_loop(0, model // step, own_product, 0)

    for n in range(NX - 1):
        share_copy(n).wait_recv()

    def normalize(m, carry):
        rows = pl.ds(pl.multiple_of(m * 32, 32), 32)
        summed = residual[rows].astype(jnp.float32) + own[rows]
        for n in range(NX - 1):
            summed += shares_in[n, rows].astype(jnp.float32)
        own[rows] = summed
        mean = jnp.mean(summed * summed, axis=-1, keepdims=True)
        normed = (summed * lax.rsqrt(mean + 1e-06) * gain_ref[...]).astype(jnp.bfloat16)
        col[0, rows] = normed[:, :wide]
        col[0, pl.ds(pl.multiple_of(TOK + m * 32, 32), 32)] = normed[:, wide:]
        return carry

    lax.fori_loop(0, TOK // 32, normalize, 0)

    place = y * NX + x
    right, left = lax.rem(z + 1, NZ), lax.rem(z + NZ - 1, NZ)

    def ring_copy(direction, n, side):
        source, target = (n - 1, n) if direction == 0 else ((NZ + 1 - n) % NZ, NZ - n)
        rows = pl.ds(side * TOK, TOK)
        return remote(
            col.at[source, rows],
            col.at[target, rows],
            col_send.at[direction, n - 1, side],
            col_recv.at[direction, n - 1, side],
            {"z": right if direction == 0 else left},
        )

    steps = [
        (n, side, direction)
        for n in range(1, 5)
        for side in range(2)
        for direction in range(2)
        if n < 4 or side == direction
    ]
    for n, side, direction in steps:
        if n == 1:
            ring_copy(direction, 1, side).start()

    def far_first(k):
        return (2 + k) * (1 - k // 2) + (3 - k) * (k // 2)

    def exchange(source, target, sends, recvs, r):
        def send(k, carry):
            device, expert = peer(far_first(k // NX) * NX + far_first(k % NX))
            remote(
                source.at[r, expert], target.at[r, place], sends.at[r], recvs.at[r], device
            ).start()
            return carry

        lax.fori_loop(0, PLANE - 1, send, 0)
        target[r, place] = source[r, place]

    def whole(source, target, sends, recvs, r):
        others = pl.ds(0, PLANE - 1)
        return remote(
            source.at[r, others], target.at[r, others], sends.at[r], recvs.at[r], {"c": c}
        )

    token = lax.broadcasted_iota(jnp.int32, (TOK, TOK), 0)
    earlier = (token < lax.broadcasted_iota(jnp.int32, (TOK, TOK), 1)).astype(jnp.bfloat16)
    expert_row = lax.broadcasted_iota(jnp.int32, (PLANE, TOK), 0) + z * PLANE
    expert_row = expert_row.astype(jnp.float32)
    slot_row = lax.rem(lax.broadcasted_iota(jnp.int32, (PLANE * 2 * CAP, TOK), 0), 2 * CAP)
    side_row = slot_row // CAP
    slot_row = lax.rem(slot_row, CAP).astype(jnp.float32)

    def slots(r):
        chosen = jnp.zeros((PLANE, TOK), jnp.float32)
        weight = jnp.zeros((PLANE, TOK), jnp.float32)
        for j in range(8):
            hit = routes_in[r, j : j + 1, :] == expert_row
            chosen = jnp.where(hit, 1.0, chosen)
            weight = jnp.where(hit, routes_in[r, 8 + j : 9 + j, :], weight)
        rank = jnp.dot(
            chosen.astype(jnp.bfloat16), earlier, preferred_element_type=jnp.float32
        )
        slot_of[r] = jnp.where(chosen > 0.0, jnp.minimum(rank, float(CAP)), float(CAP))
        weight_of[r] = weight

    def by_slot(values):
        rows = jnp.broadcast_to(values[:, None, :], (PLANE, 2 * CAP, TOK))
        return rows.reshape(PLANE * 2 * CAP, TOK)

    def taken(r):
        return by_slot(slot_of[r]) == slot_row

    def both_sides(values):
        low, high = jnp.where(side_row == 0, values, 0.0), jnp.where(side_row == 1, values, 0.0)
        return jnp.concatenate([low, high], axis=1)

    def dispatch(r):
        slots(r)
        pick = both_sides(jnp.where(taken(r), 1.0, 0.0)).astype(jnp.bfloat16)

        def select(n, carry):
            columns = pl.ds(pl.multiple_of(n * step, step), step)
            rows = jnp.dot(pick, col[r, :, columns], preferred_element_type=jnp.float32)
            stage[r, :, :, columns] = rows.reshape(PLANE, 2 * CAP, step).astype(jnp.bfloat16)
            return carry

        lax.fori_loop(0, wide // step, select, 0)
        exchange(stage, recv, out_send, out_recv, r)

    def expert(blocks):
        rows = []
        for r in blocks:
            whole(stage, recv, out_send, out_recv, r).wait_recv()
            came = recv[r].astype(jnp.float32).reshape(PLANE, 2, CAP, wide)
            sides = [came[:, side].reshape(PLANE * CAP, wide) for side in range(2)]
            rows.append(jnp.concatenate(sides, axis=1).astype(jnp.bfloat16))
        rows = jnp.concatenate(rows, axis=0) if len(rows) > 1 else rows[0]
        width = w_out.shape[1]
        acts = []
        for p in range(2):
            gate_up = jnp.dot(rows, w_in[p], preferred_element_type=jnp.float32)
            gate, up = gate_up[:, :width], gate_up[:, width:]
            acts.append((gate / (1.0 + jnp.exp(-gate)) * up).astype(jnp.bfloat16))

        def down(n, carry):
            sides = []
            for side in range(2):
                columns = pl.ds(pl.multiple_of(side * wide + n * step, step), step)
                total = jnp.dot(acts[0], w_out[0, :, columns], preferred_element_type=jnp.float32)
                total += jnp.dot(acts[1], w_out[1, :, columns], preferred_element_type=jnp.float32)
                sides.append(total.reshape(len(blocks), PLANE, 1, CAP, step))
            total = jnp.concatenate(sides, axis=2).reshape(len(blocks), PLANE, 2 * CAP, step)
            columns = pl.ds(pl.multiple_of(n * step, step), step)
            for i, r in enumerate(blocks):
                recv[r, :, :, columns] = total[i].astype(jnp.bfloat16)
            return carry

        lax.fori_loop(0, wide // step, down, 0)

    routes_in[0] = routes_ref[...]
    for d in range(1, NZ):
        route_copy(d).wait()

    dispatch(0)

    groups = [(0,), (1, 7), (2, 6), (3, 5), (4,)]
    for n in range(1, 5):
        for at, side, direction in steps:
            if at == n:
                ring_copy(direction, n, side).wait_recv()
                if (n + 1, side, direction) in steps:
                    ring_copy(direction, n + 1, side).start()
        for r in groups[n]:
            dispatch(r)
        if n == 1:
            for copy in weight_copies:
                copy.wait()
        expert(groups[n - 1])
    expert(groups[4])

    def give_back(n):
        for r in groups[n]:
            exchange(recv, back, back_send, back_recv, r)

    def sum_copy(direction, n, side):
        source, target = (n, n - 1) if direction == 0 else (NZ - n, NZ + 1 - n)
        rows = pl.ds(side * TOK, TOK)
        return remote(
            acc.at[source, rows],
            ring.at[target, rows],
            ring_send.at[direction, n - 1, side],
            ring_recv.at[direction, n - 1, side],
            {"z": left if direction == 0 else right},
        )

    def weigh(r, sums):
        spread = both_sides(jnp.where(taken(r), by_slot(weight_of[r]), 0.0))
        high = spread.astype(jnp.bfloat16)
        low = (spread - high.astype(jnp.float32)).astype(jnp.bfloat16)

        def part(n, carry):
            columns = pl.ds(pl.multiple_of(n * step, step), step)
            rows = back[r, :, :, columns].reshape(PLANE * 2 * CAP, step)
            total = jnp.zeros((2 * TOK, step), jnp.float32)
            for matrix in (high, low):
                total += lax.dot_general(
                    matrix, rows, (((0,), (0,)), ((), ())), preferred_element_type=jnp.float32
                )
            sums[:, columns] = total
            return carry

        lax.fori_loop(0, wide // step, part, 0)

    give_back(4)
    give_back(3)
    for n in (4, 3, 2, 1, 0):
        for k, r in enumerate(groups[n]):
            whole(recv, back, back_send, back_recv, r).wait_recv()
            weigh(r, home.at[k])
        if n == 0:
            break
        for at, side, direction in steps:
            if at != n:
                continue
            r = n if direction == 0 else NZ - n
            rows = pl.ds(side * TOK, TOK)
            total = home[0 if n == 4 else direction, rows]
            if (n + 1, side, direction) in steps:
                sum_copy(direction, n + 1, side).wait_recv()
                total += ring[r, rows].astype(jnp.float32)
            acc[r, rows] = total.astype(jnp.bfloat16)
            sum_copy(direction, n, side).start()
        if n >= 2:
            give_back(n - 2)

    for side in range(2):
        rows = pl.ds(side * TOK, TOK)
        columns = pl.ds(side * wide, wide)
        moe_sum = home[0, rows]
        for direction in range(2):
            sum_copy(direction, 1, side).wait_recv()
            moe_sum += ring[direction * NZ, rows].astype(jnp.float32)
        out_ref[:, columns] = (own[:, columns] + moe_sum).astype(jnp.bfloat16)

    for r in range(NZ):
        whole(stage, recv, out_send, out_recv, r).wait_send()
        whole(recv, back, back_send, back_recv, r).wait_send()
    for n, side, direction in steps:
        ring_copy(direction, n, side).wait_send()
        sum_copy(direction, n, side).wait_send()

    def drain(g, carry):
        for number in (1, 2):
            hop(g, number).wait_send()
        for d in range(1, NY):
            to_row(g, 1, d).wait_send()

            @pl.when(y + d < NY)
            def _():
                to_row(g, 2, d).wait_send()

            @pl.when(y + d >= NY)
            def _():
                to_row(g, 0, d).wait_send()

        return carry

    lax.fori_loop(0, KVH, drain, 0)
    for n in range(NX - 1):
        attend_copy(n).wait_send()
        share_copy(n).wait_send()


def layer(
    queries, kv, key_docs, query_docs, routes, residual, gain, out_weight, expert_in, expert_out
):
    model = residual.shape[1]
    vmem, hbm = pl.BlockSpec(memory_space=pltpu.VMEM), pl.BlockSpec(memory_space=pl.ANY)
    dma = pltpu.SemaphoreType.DMA
    half = HEADS * HD // NX
    bf16, f32 = jnp.bfloat16, jnp.float32
    slots = (NZ, PLANE, 2 * CAP, model // 2)
    blocks = (NZ, 2 * TOK, model // 2)
    return pl.pallas_call(
        layer_kernel,
        out_shape=jax.ShapeDtypeStruct(residual.shape, bf16),
        in_specs=[hbm, vmem, vmem, vmem, vmem, hbm, vmem, hbm, hbm, hbm],
        out_specs=vmem,
        scratch_shapes=[
            pltpu.VMEM(queries.shape, bf16),
            pltpu.VMEM(residual.shape, bf16),
            pltpu.VMEM((TOK, SPAN), f32),
            pltpu.VMEM((KVH, 3 * NY, TOK, 2 * HD), bf16),
            pltpu.VMEM((KVH, TOK, half), bf16),
            pltpu.VMEM((NX, TOK, half), bf16),
            pltpu.VMEM((NC,) + out_weight.shape, bf16),
            pltpu.VMEM((NX - 1, TOK, model), bf16),
            pltpu.VMEM((NX - 1, TOK, model), bf16),
            pltpu.VMEM((TOK, model), f32),
            pltpu.VMEM((NZ,) + routes.shape, f32),
            pltpu.VMEM(blocks, bf16),
            pltpu.VMEM(slots, bf16),
            pltpu.VMEM(slots, bf16),
            pltpu.VMEM(slots, bf16),
            pltpu.VMEM(blocks, bf16),
            pltpu.VMEM((NZ + 1,) + blocks[1:], bf16),
            pltpu.VMEM((2,) + blocks[1:], f32),
            pltpu.VMEM((NZ, PLANE, TOK), f32),
            pltpu.VMEM((NZ, PLANE, TOK), f32),
            pltpu.VMEM((2,) + expert_in.shape[1:], bf16),
            pltpu.VMEM((2,) + expert_out.shape[1:], bf16),
            dma((3,)),
            dma,
            dma,
            dma((NZ,)),
            dma((NZ,)),
            dma((KVH, 2)),
            dma((KVH, 2)),
            dma((KVH, 3, NY - 1)),
            dma((KVH, 3, NY - 1)),
            dma((NX - 1,)),
            dma((NX - 1,)),
            dma((NX - 1,)),
            dma((NX - 1,)),
            dma((2,)),
            dma((2,)),
            dma((2,)),
            dma((2, 4, 2)),
            dma((2, 4, 2)),
            dma((NZ,)),
            dma((NZ,)),
            dma((NZ,)),
            dma((NZ,)),
            dma((2, 4, 2)),
            dma((2, 4, 2)),
        ],
        compiler_params=pltpu.CompilerParams(
            collective_id=1, has_side_effects=True, vmem_limit_bytes=60 * 2**20
        ),
        cost_estimate=pl.CostEstimate(
            flops=14 * 10**9, bytes_accessed=20 * 2**20, transcendentals=HEADS * TOK * SPAN
        ),
        name="layer",
    )(queries, kv, key_docs, query_docs, routes, residual, gain, out_weight, expert_in, expert_out)


def on_device(
    queries,
    keyvals,
    residual,
    out_weight,
    norm_gain,
    doc_ids,
    expert_ids,
    route_weights,
    expert_in,
    expert_out,
):
    number = ((lax.axis_index("x") * NC + lax.axis_index("c")) * NZ + lax.axis_index("z")) * NY
    number += lax.axis_index("y")
    padded = jnp.concatenate([jnp.full((DOC_MAX,), -1, jnp.int32), doc_ids], axis=0)
    key_docs = lax.dynamic_slice_in_dim(padded, number * TOK, SPAN, 0)
    routes = jnp.concatenate([expert_ids.astype(jnp.float32), route_weights], axis=1).T
    return layer(
        queries,
        keyvals.transpose(1, 0, 2),
        key_docs[None, :],
        key_docs[DOC_MAX:, None],
        routes,
        residual,
        norm_gain[None],
        out_weight,
        expert_in,
        expert_out,
    )


def solution(mesh):
    torus = Mesh(mesh.devices.reshape(NZ, NY, NX, NC), ("z", "y", "x", "c"))
    tokens = ("x", "c", "z", "y")
    experts = ("z", "y", "x", "c")
    placed = (
        P(tokens, None),
        P(tokens, None, None),
        P(tokens, None),
        P(("x", "c"), None),
        P(),
        P(),
        P(tokens, None),
        P(tokens, None),
        P(experts, None, None),
        P(experts, None, None),
    )
    return jax.shard_map(
        on_device, mesh=torus, in_specs=placed, out_specs=P(tokens, None), check_vma=False
    )
```

```python
import math

import jax
import jax.numpy as jnp
from jax import lax
from jax.experimental import pallas as pl
from jax.experimental.pallas import tpu as pltpu
from jax.sharding import Mesh, PartitionSpec as P

NZ, NY, NX, NC = 8, 4, 4, 2
TOK = 128
HD = 128
KVH = 4
HEADS = 32
GROUP = HEADS // KVH
HG = 4
CAP = 8
DOC_MAX = 1024
SPAN = DOC_MAX + TOK
MESH_AXES = ("z", "y", "x", "c")
COUNT = NZ * NY * NX * NC
PLANE = NY * NX
MESH = pl.DeviceIdType.MESH


def layer_kernel(
    queries_hbm,
    kv_ref,
    key_docs_ref,
    query_docs_ref,
    routes_ref,
    residual_hbm,
    gain_ref,
    weight_hbm,
    w_in_hbm,
    w_out_hbm,
    out_ref,
    queries,
    residual,
    bias,
    bias_middle,
    bias_outer,
    stats,
    window,
    attended,
    arrived,
    weight,
    share,
    shares_in,
    own,
    routes_in,
    col,
    stage,
    recv,
    back,
    acc,
    ring,
    home,
    slot_of,
    weight_of,
    w_in,
    w_out,
    load_sem,
    given_send,
    given_recv,
    route_send,
    route_recv,
    z_send,
    z_recv,
    y_send,
    y_recv,
    att_send,
    att_recv,
    share_send,
    share_recv,
    own_sem,
    w_send,
    w_recv,
    col_send,
    col_recv,
    out_send,
    out_recv,
    back_send,
    back_recv,
    ring_send,
    ring_recv,
):
    z, y, x, c = (lax.axis_index(name) for name in MESH_AXES)
    model = residual.shape[1]
    wide = model // 2
    scale = math.log2(math.e) / math.sqrt(HD)

    cp = x * NC + c
    wrap = (z + 1) // NZ
    cp_ahead = lax.rem(cp + wrap, NX * NC)
    ahead = {"z": lax.rem(z + 1, NZ), "x": cp_ahead // NC, "c": lax.rem(cp_ahead, NC)}
    wrap = 1 - (z + NZ - 1) // NZ
    cp_behind = lax.rem(cp + NX * NC - wrap, NX * NC)
    behind = {
        "z": lax.rem(z + NZ - 1, NZ),
        "x": cp_behind // NC,
        "c": lax.rem(cp_behind, NC),
    }

    def along(axis, position, distance, size):
        return {axis: lax.rem(position + distance, size)}

    def peer(k):
        other_y, other_x = lax.rem(y + k // NX, NY), lax.rem(x + k % NX, NX)
        return {"y": other_y, "x": other_x}, other_y * NX + other_x

    barrier = pltpu.get_barrier_semaphore()

    def greet(k, carry):
        pl.semaphore_signal(barrier, inc=1, device_id=peer(k)[0], device_id_type=MESH)
        return carry

    lax.fori_loop(1, PLANE, greet, 0)
    others = [ahead, behind, {"c": 1 - c}]
    others += [along("z", z, d, NZ) for d in range(1, NZ)]
    for other in others:
        pl.semaphore_signal(barrier, inc=1, device_id=other, device_id_type=MESH)
    pl.semaphore_wait(barrier, PLANE - 1 + len(others))

    def remote(source, target, send, recv, device):
        return pltpu.make_async_remote_copy(
            src_ref=source,
            dst_ref=target,
            send_sem=send,
            recv_sem=recv,
            device_id=device,
            device_id_type=MESH,
        )

    def hop(g, number):
        source = window.at[g, (3 - number) * NY + y]
        target = window.at[g, (2 - number) * NY + y]
        return remote(
            source, target, z_send.at[g, number - 1], z_recv.at[g, number - 1], ahead
        )

    def to_row(g, plane, d):
        block = window.at[g, plane * NY + y]
        return remote(
            block,
            block,
            y_send.at[g, plane, d - 1],
            y_recv.at[g, plane, d - 1],
            along("y", y, d, NY),
        )

    def route_copy(d):
        return remote(
            routes_ref,
            routes_in.at[d],
            route_send.at[d],
            route_recv.at[d],
            along("z", z, d, NZ),
        )

    def rotated(n):
        return lax.rem(x + 1 + n, KVH)

    def first(n, carry):
        g = rotated(n)
        window[g, 2 * NY + y] = kv_ref[g]
        hop(g, 1).start()
        for d in range(1, NY):

            @pl.when(y + d < NY)
            def _():
                to_row(g, 2, d).start()

        return carry

    lax.fori_loop(0, KVH, first, 0)

    for d in range(1, NZ):
        route_copy(d).start()
    loads = [
        pltpu.make_async_copy(queries_hbm, queries, load_sem.at[0]),
        pltpu.make_async_copy(residual_hbm, residual, load_sem.at[1]),
        pltpu.make_async_copy(weight_hbm, weight.at[c], load_sem.at[2]),
        remote(weight_hbm, weight.at[c], given_send, given_recv, {"c": 1 - c}),
    ]
    for load in loads:
        load.start()

    def second(n, carry):
        g = rotated(n)
        hop(g, 1).wait_recv()
        hop(g, 2).start()
        for d in range(1, NY):
            to_row(g, 1, d).start()
        return carry

    lax.fori_loop(0, KVH, second, 0)

    keys_at = lax.broadcasted_iota(jnp.int32, (TOK, SPAN), 1)
    tokens_at = lax.broadcasted_iota(jnp.int32, (TOK, SPAN), 0) + DOC_MAX
    allowed = (key_docs_ref[...] == query_docs_ref[...]) & (keys_at <= tokens_at)
    bias[...] = jnp.where(allowed, 0.0, -1e30)

    middle = pl.ds(pl.multiple_of((NY - y) * TOK, TOK), NY * TOK)
    bias_middle[...] = bias[:, middle]

    def outer_block(b):
        return b + NY * ((y + b) // NY)

    for b in range(NY + 1):
        at = pl.ds(pl.multiple_of(outer_block(b) * TOK, TOK), TOK)
        bias_outer[:, b * TOK : (b + 1) * TOK] = bias[:, at]

    def third(n, carry):
        g = rotated(n)
        hop(g, 2).wait_recv()
        for d in range(1, NY):

            @pl.when(y + d >= NY)
            def _():
                to_row(g, 0, d).start()

        return carry

    lax.fori_loop(0, KVH, third, 0)

    weight_copies = []
    for n, (hbm, vmem) in enumerate(((w_in_hbm, w_in), (w_out_hbm, w_out))):
        own_part = pltpu.make_async_copy(hbm.at[0], vmem.at[c], own_sem.at[n])
        given = remote(hbm.at[0], vmem.at[c], w_send.at[n], w_recv.at[n], {"c": 1 - c})
        own_part.start()
        given.start()
        weight_copies += [own_part, given]

    for load in loads:
        load.wait()

    def attend_copy(n):
        g = rotated(n)
        return remote(
            attended.at[g], arrived.at[x], att_send.at[n], att_recv.at[n], {"x": g}
        )

    def source_of(n):
        return lax.rem(x + NX - 1 - n, NX)

    def share_copy(n):
        source = source_of(n)
        return remote(
            share.at[n], shares_in.at[n], share_send.at[n], share_recv.at[n], {"x": source}
        )

    step = 512

    def product(rows, columns):
        total = jnp.dot(rows[:, : HG * HD], weight[0, :, columns], preferred_element_type=jnp.float32)
        total += jnp.dot(rows[:, HG * HD :], weight[1, :, columns], preferred_element_type=jnp.float32)
        return total

    def project(n):
        attend_copy(n).wait_recv()
        rows = arrived[source_of(n)]

        def part(m, carry):
            columns = pl.ds(pl.multiple_of(m * step, step), step)
            share[n, :, columns] = product(rows, columns).astype(jnp.bfloat16)
            return carry

        lax.fori_loop(0, model // step, part, 0)
        share_copy(n).start()

    def two_queries(g, i):
        first_column = g * GROUP * HD + i * HD
        return jnp.concatenate(
            [queries[:, pl.ds(pl.multiple_of(first_column + k * HD, HD), HD)] for k in range(2)],
            axis=0,
        )

    def score(q, keys, added):
        scores = lax.dot_general(
            q, keys, (((1,), (1,)), ((), ())), preferred_element_type=jnp.float32
        )
        return scores.reshape(2, TOK, keys.shape[0]) * scale + added

    def weighted(exponent, values):
        rows = exponent.astype(jnp.bfloat16).reshape(2 * TOK, values.shape[0])
        total = jnp.dot(rows, values, preferred_element_type=jnp.float32)
        return total.reshape(2, TOK, HD)

    low_lanes = lax.broadcasted_iota(jnp.int32, (TOK, HD), 1) < HD // 2

    def middle_part(n, carry):
        g = rotated(n)
        for d in range(1, NY):
            to_row(g, 1, d).wait_recv()
        block = window[g, NY : 2 * NY].reshape(NY * TOK, 2 * HD)
        keys, values = block[:, :HD], block[:, HD:]
        for i in range(0, GROUP, 2):
            scores = score(two_queries(g, i), keys, bias_middle[...])
            top = jnp.max(scores, axis=-1, keepdims=True)
            exponent = jnp.exp2(scores - top)
            denominator = jnp.sum(exponent, axis=-1, keepdims=True)
            numerator = weighted(exponent, values)
            for k in range(2):
                rows = pl.ds(pl.multiple_of(lax.rem(g, 2) * TOK, TOK), TOK)
                home[g // 2, rows, (i + k) * HD : (i + k + 1) * HD] = numerator[k]
                stats[g, i + k] = jnp.where(low_lanes, top[k], denominator[k])
        return carry

    lax.fori_loop(0, KVH, middle_part, 0)

    def one_kv_head(n, carry):
        g = rotated(n)
        for d in range(1, NY):

            @pl.when(y >= d)
            def _():
                to_row(g, 2, d).wait_recv()

            @pl.when(y < d)
            def _():
                to_row(g, 0, d).wait_recv()

        blocks = [window[g, y + outer_block(b)] for b in range(NY + 1)]
        keys = jnp.concatenate([block[:, :HD] for block in blocks], axis=0)
        values = jnp.concatenate([block[:, HD:] for block in blocks], axis=0)
        for i in range(0, GROUP, 2):
            scores = score(two_queries(g, i), keys, bias_outer[...])
            rows = pl.ds(pl.multiple_of(lax.rem(g, 2) * TOK, TOK), TOK)
            before = [home[g // 2, rows, (i + k) * HD : (i + k + 1) * HD] for k in range(2)]
            before_top = jnp.stack([stats[g, i + k][:, :1] for k in range(2)])
            before_sum = jnp.stack([stats[g, i + k][:, HD // 2 : HD // 2 + 1] for k in range(2)])
            top = jnp.maximum(jnp.max(scores, axis=-1, keepdims=True), before_top)
            exponent = jnp.exp2(scores - top)
            factor = jnp.exp2(before_top - top)
            denominator = jnp.sum(exponent, axis=-1, keepdims=True) + factor * before_sum
            numerator = weighted(exponent, values) + factor * jnp.stack(before)
            result = (numerator / denominator).astype(jnp.bfloat16)
            for k in range(2):
                attended[g, :, (i + k) * HD : (i + k + 1) * HD] = result[k]

        @pl.when(n < NX - 1)
        def _():
            attend_copy(n).start()

        @pl.when(n > 0)
        def _():
            project(n - 1)

        return carry

    lax.fori_loop(0, KVH, one_kv_head, 0)

    mine = attended[x]

    def own_product(m, carry):
        columns = pl.ds(pl.multiple_of(m * step, step), step)
        own[:, columns] = product(mine, columns)
        return carry

    lax.fori_loop(0, model // step, own_product, 0)

    for n in range(NX - 1):
        share_copy(n).wait_recv()

    def normalize(m, carry):
        rows = pl.ds(pl.multiple_of(m * 32, 32), 32)
        summed = residual[rows].astype(jnp.float32) + own[rows]
        for n in range(NX - 1):
            summed += shares_in[n, rows].astype(jnp.float32)
        own[rows] = summed
        mean = jnp.mean(summed * summed, axis=-1, keepdims=True)
        normed = (summed * lax.rsqrt(mean + 1e-06) * gain_ref[...]).astype(jnp.bfloat16)
        col[0, rows] = normed[:, :wide]
        col[0, pl.ds(pl.multiple_of(TOK + m * 32, 32), 32)] = normed[:, wide:]
        return carry

    lax.fori_loop(0, TOK // 32, normalize, 0)

    place = y * NX + x
    right, left = lax.rem(z + 1, NZ), lax.rem(z + NZ - 1, NZ)

    def ring_copy(direction, n, side):
        source, target = (n - 1, n) if direction == 0 else ((NZ + 1 - n) % NZ, NZ - n)
        rows = pl.ds(side * TOK, TOK)
        return remote(
            col.at[source, rows],
            col.at[target, rows],
            col_send.at[direction, n - 1, side],
            col_recv.at[direction, n - 1, side],
            {"z": right if direction == 0 else left},
        )

    steps = [
        (n, side, direction)
        for n in range(1, 5)
        for side in range(2)
        for direction in range(2)
        if n < 4 or side == direction
    ]
    for n, side, direction in steps:
        if n == 1:
            ring_copy(direction, 1, side).start()

    def far_first(k):
        return (2 + k) * (1 - k // 2) + (3 - k) * (k // 2)

    def exchange(source, target, sends, recvs, r):
        def send(k, carry):
            device, expert = peer(far_first(k // NX) * NX + far_first(k % NX))
            remote(
                source.at[r, expert], target.at[r, place], sends.at[r], recvs.at[r], device
            ).start()
            return carry

        lax.fori_loop(0, PLANE - 1, send, 0)
        target[r, place] = source[r, place]

    def whole(source, target, sends, recvs, r):
        others = pl.ds(0, PLANE - 1)
        return remote(
            source.at[r, others], target.at[r, others], sends.at[r], recvs.at[r], {"c": c}
        )

    token = lax.broadcasted_iota(jnp.int32, (TOK, TOK), 0)
    earlier = (token < lax.broadcasted_iota(jnp.int32, (TOK, TOK), 1)).astype(jnp.bfloat16)
    expert_row = lax.broadcasted_iota(jnp.int32, (PLANE, TOK), 0) + z * PLANE
    expert_row = expert_row.astype(jnp.float32)
    slot_row = lax.rem(lax.broadcasted_iota(jnp.int32, (PLANE * 2 * CAP, TOK), 0), 2 * CAP)
    side_row = slot_row // CAP
    slot_row = lax.rem(slot_row, CAP).astype(jnp.float32)

    def slots(r):
        chosen = jnp.zeros((PLANE, TOK), jnp.float32)
        weight = jnp.zeros((PLANE, TOK), jnp.float32)
        for j in range(8):
            hit = routes_in[r, j : j + 1, :] == expert_row
            chosen = jnp.where(hit, 1.0, chosen)
            weight = jnp.where(hit, routes_in[r, 8 + j : 9 + j, :], weight)
        rank = jnp.dot(
            chosen.astype(jnp.bfloat16), earlier, preferred_element_type=jnp.float32
        )
        slot_of[r] = jnp.where(chosen > 0.0, jnp.minimum(rank, float(CAP)), float(CAP))
        weight_of[r] = weight

    def by_slot(values):
        rows = jnp.broadcast_to(values[:, None, :], (PLANE, 2 * CAP, TOK))
        return rows.reshape(PLANE * 2 * CAP, TOK)

    def taken(r):
        return by_slot(slot_of[r]) == slot_row

    def both_sides(values):
        low, high = jnp.where(side_row == 0, values, 0.0), jnp.where(side_row == 1, values, 0.0)
        return jnp.concatenate([low, high], axis=1)

    def dispatch(r):
        slots(r)
        pick = both_sides(jnp.where(taken(r), 1.0, 0.0)).astype(jnp.bfloat16)

        def select(n, carry):
            columns = pl.ds(pl.multiple_of(n * step, step), step)
            rows = jnp.dot(pick, col[r, :, columns], preferred_element_type=jnp.float32)
            stage[r, :, :, columns] = rows.reshape(PLANE, 2 * CAP, step).astype(jnp.bfloat16)
            return carry

        lax.fori_loop(0, wide // step, select, 0)
        exchange(stage, recv, out_send, out_recv, r)

    def expert(blocks):
        rows = []
        for r in blocks:
            whole(stage, recv, out_send, out_recv, r).wait_recv()
            came = recv[r].astype(jnp.float32).reshape(PLANE, 2, CAP, wide)
            sides = [came[:, side].reshape(PLANE * CAP, wide) for side in range(2)]
            rows.append(jnp.concatenate(sides, axis=1).astype(jnp.bfloat16))
        rows = jnp.concatenate(rows, axis=0) if len(rows) > 1 else rows[0]
        width = w_out.shape[1]
        acts = []
        for p in range(2):
            gate_up = jnp.dot(rows, w_in[p], preferred_element_type=jnp.float32)
            gate, up = gate_up[:, :width], gate_up[:, width:]
            acts.append((gate / (1.0 + jnp.exp(-gate)) * up).astype(jnp.bfloat16))

        def down(n, carry):
            sides = []
            for side in range(2):
                columns = pl.ds(pl.multiple_of(side * wide + n * step, step), step)
                total = jnp.dot(acts[0], w_out[0, :, columns], preferred_element_type=jnp.float32)
                total += jnp.dot(acts[1], w_out[1, :, columns], preferred_element_type=jnp.float32)
                sides.append(total.reshape(len(blocks), PLANE, 1, CAP, step))
            total = jnp.concatenate(sides, axis=2).reshape(len(blocks), PLANE, 2 * CAP, step)
            columns = pl.ds(pl.multiple_of(n * step, step), step)
            for i, r in enumerate(blocks):
                recv[r, :, :, columns] = total[i].astype(jnp.bfloat16)
            return carry

        lax.fori_loop(0, wide // step, down, 0)

    routes_in[0] = routes_ref[...]
    for d in range(1, NZ):
        route_copy(d).wait()

    dispatch(0)

    groups = [(0,), (1, 7), (2, 6), (3, 5), (4,)]
    for n in range(1, 5):
        for at, side, direction in steps:
            if at == n:
                ring_copy(direction, n, side).wait_recv()
                if (n + 1, side, direction) in steps:
                    ring_copy(direction, n + 1, side).start()
        for r in groups[n]:
            dispatch(r)
        if n == 1:
            for copy in weight_copies:
                copy.wait()
        expert(groups[n - 1])
    expert(groups[4])

    def give_back(n):
        for r in groups[n]:
            exchange(recv, back, back_send, back_recv, r)

    def sum_copy(direction, n, side):
        source, target = (n, n - 1) if direction == 0 else (NZ - n, NZ + 1 - n)
        rows = pl.ds(side * TOK, TOK)
        return remote(
            acc.at[source, rows],
            ring.at[target, rows],
            ring_send.at[direction, n - 1, side],
            ring_recv.at[direction, n - 1, side],
            {"z": left if direction == 0 else right},
        )

    def weigh(r, sums):
        spread = both_sides(jnp.where(taken(r), by_slot(weight_of[r]), 0.0))
        high = spread.astype(jnp.bfloat16)
        low = (spread - high.astype(jnp.float32)).astype(jnp.bfloat16)

        def part(n, carry):
            columns = pl.ds(pl.multiple_of(n * step, step), step)
            rows = back[r, :, :, columns].reshape(PLANE * 2 * CAP, step)
            total = jnp.zeros((2 * TOK, step), jnp.float32)
            for matrix in (high, low):
                total += lax.dot_general(
                    matrix, rows, (((0,), (0,)), ((), ())), preferred_element_type=jnp.float32
                )
            sums[:, columns] = total
            return carry

        lax.fori_loop(0, wide // step, part, 0)

    give_back(4)
    give_back(3)
    for n in (4, 3, 2, 1, 0):
        for k, r in enumerate(groups[n]):
            whole(recv, back, back_send, back_recv, r).wait_recv()
            weigh(r, home.at[k])
        if n == 0:
            break
        for at, side, direction in steps:
            if at != n:
                continue
            r = n if direction == 0 else NZ - n
            rows = pl.ds(side * TOK, TOK)
            total = home[0 if n == 4 else direction, rows]
            if (n + 1, side, direction) in steps:
                sum_copy(direction, n + 1, side).wait_recv()
                total += ring[r, rows].astype(jnp.float32)
            acc[r, rows] = total.astype(jnp.bfloat16)
            sum_copy(direction, n, side).start()
        if n >= 2:
            give_back(n - 2)

    for side in range(2):
        rows = pl.ds(side * TOK, TOK)
        columns = pl.ds(side * wide, wide)
        moe_sum = home[0, rows]
        for direction in range(2):
            sum_copy(direction, 1, side).wait_recv()
            moe_sum += ring[direction * NZ, rows].astype(jnp.float32)
        out_ref[:, columns] = (own[:, columns] + moe_sum).astype(jnp.bfloat16)

    for r in range(NZ):
        whole(stage, recv, out_send, out_recv, r).wait_send()
        whole(recv, back, back_send, back_recv, r).wait_send()
    for n, side, direction in steps:
        ring_copy(direction, n, side).wait_send()
        sum_copy(direction, n, side).wait_send()

    def drain(g, carry):
        for number in (1, 2):
            hop(g, number).wait_send()
        for d in range(1, NY):
            to_row(g, 1, d).wait_send()

            @pl.when(y + d < NY)
            def _():
                to_row(g, 2, d).wait_send()

            @pl.when(y + d >= NY)
            def _():
                to_row(g, 0, d).wait_send()

        return carry

    lax.fori_loop(0, KVH, drain, 0)
    for n in range(NX - 1):
        attend_copy(n).wait_send()
        share_copy(n).wait_send()


def layer(
    queries, kv, key_docs, query_docs, routes, residual, gain, out_weight, expert_in, expert_out
):
    model = residual.shape[1]
    vmem, hbm = pl.BlockSpec(memory_space=pltpu.VMEM), pl.BlockSpec(memory_space=pl.ANY)
    dma = pltpu.SemaphoreType.DMA
    half = HEADS * HD // NX
    bf16, f32 = jnp.bfloat16, jnp.float32
    slots = (NZ, PLANE, 2 * CAP, model // 2)
    blocks = (NZ, 2 * TOK, model // 2)
    return pl.pallas_call(
        layer_kernel,
        out_shape=jax.ShapeDtypeStruct(residual.shape, bf16),
        in_specs=[hbm, vmem, vmem, vmem, vmem, hbm, vmem, hbm, hbm, hbm],
        out_specs=vmem,
        scratch_shapes=[
            pltpu.VMEM(queries.shape, bf16),
            pltpu.VMEM(residual.shape, bf16),
            pltpu.VMEM((TOK, SPAN), f32),
            pltpu.VMEM((TOK, NY * TOK), f32),
            pltpu.VMEM((TOK, (NY + 1) * TOK), f32),
            pltpu.VMEM((KVH, GROUP, TOK, HD), f32),
            pltpu.VMEM((KVH, 3 * NY, TOK, 2 * HD), bf16),
            pltpu.VMEM((KVH, TOK, half), bf16),
            pltpu.VMEM((NX, TOK, half), bf16),
            pltpu.VMEM((NC,) + out_weight.shape, bf16),
            pltpu.VMEM((NX - 1, TOK, model), bf16),
            pltpu.VMEM((NX - 1, TOK, model), bf16),
            pltpu.VMEM((TOK, model), f32),
            pltpu.VMEM((NZ,) + routes.shape, f32),
            pltpu.VMEM(blocks, bf16),
            pltpu.VMEM(slots, bf16),
            pltpu.VMEM(slots, bf16),
            pltpu.VMEM(slots, bf16),
            pltpu.VMEM(blocks, bf16),
            pltpu.VMEM((NZ + 1,) + blocks[1:], bf16),
            pltpu.VMEM((2,) + blocks[1:], f32),
            pltpu.VMEM((NZ, PLANE, TOK), f32),
            pltpu.VMEM((NZ, PLANE, TOK), f32),
            pltpu.VMEM((2,) + expert_in.shape[1:], bf16),
            pltpu.VMEM((2,) + expert_out.shape[1:], bf16),
            dma((3,)),
            dma,
            dma,
            dma((NZ,)),
            dma((NZ,)),
            dma((KVH, 2)),
            dma((KVH, 2)),
            dma((KVH, 3, NY - 1)),
            dma((KVH, 3, NY - 1)),
            dma((NX - 1,)),
            dma((NX - 1,)),
            dma((NX - 1,)),
            dma((NX - 1,)),
            dma((2,)),
            dma((2,)),
            dma((2,)),
            dma((2, 4, 2)),
            dma((2, 4, 2)),
            dma((NZ,)),
            dma((NZ,)),
            dma((NZ,)),
            dma((NZ,)),
            dma((2, 4, 2)),
            dma((2, 4, 2)),
        ],
        compiler_params=pltpu.CompilerParams(
            collective_id=1, has_side_effects=True, vmem_limit_bytes=60 * 2**20
        ),
        cost_estimate=pl.CostEstimate(
            flops=14 * 10**9, bytes_accessed=20 * 2**20, transcendentals=HEADS * TOK * SPAN
        ),
        name="layer",
    )(queries, kv, key_docs, query_docs, routes, residual, gain, out_weight, expert_in, expert_out)


def on_device(
    queries,
    keyvals,
    residual,
    out_weight,
    norm_gain,
    doc_ids,
    expert_ids,
    route_weights,
    expert_in,
    expert_out,
):
    number = ((lax.axis_index("x") * NC + lax.axis_index("c")) * NZ + lax.axis_index("z")) * NY
    number += lax.axis_index("y")
    padded = jnp.concatenate([jnp.full((DOC_MAX,), -1, jnp.int32), doc_ids], axis=0)
    key_docs = lax.dynamic_slice_in_dim(padded, number * TOK, SPAN, 0)
    routes = jnp.concatenate([expert_ids.astype(jnp.float32), route_weights], axis=1).T
    return layer(
        queries,
        keyvals.transpose(1, 0, 2),
        key_docs[None, :],
        key_docs[DOC_MAX:, None],
        routes,
        residual,
        norm_gain[None],
        out_weight,
        expert_in,
        expert_out,
    )


def solution(mesh):
    torus = Mesh(mesh.devices.reshape(NZ, NY, NX, NC), ("z", "y", "x", "c"))
    tokens = ("x", "c", "z", "y")
    experts = ("z", "y", "x", "c")
    placed = (
        P(tokens, None),
        P(tokens, None, None),
        P(tokens, None),
        P(("x", "c"), None),
        P(),
        P(),
        P(tokens, None),
        P(tokens, None),
        P(experts, None, None),
        P(experts, None, None),
    )
    return jax.shard_map(
        on_device, mesh=torus, in_specs=placed, out_specs=P(tokens, None), check_vma=False
    )
```

```python
import math

import jax
import jax.numpy as jnp
from jax import lax
from jax.experimental import pallas as pl
from jax.experimental.pallas import tpu as pltpu
from jax.sharding import Mesh, PartitionSpec as P

NZ, NY, NX, NC = 8, 4, 4, 2
TOK = 128
HD = 128
KVH = 4
HEADS = 32
GROUP = HEADS // KVH
HG = 4
CAP = 8
DOC_MAX = 1024
SPAN = DOC_MAX + TOK
MESH_AXES = ("z", "y", "x", "c")
COUNT = NZ * NY * NX * NC
PLANE = NY * NX
MESH = pl.DeviceIdType.MESH


def layer_kernel(
    queries_hbm,
    kv_ref,
    key_docs_ref,
    query_docs_ref,
    routes_ref,
    residual_hbm,
    gain_ref,
    weight_hbm,
    w_in_hbm,
    w_out_hbm,
    out_ref,
    queries,
    residual,
    bias,
    bias_middle,
    bias_outer,
    stats,
    window,
    attended,
    arrived,
    weight,
    share,
    shares_in,
    own,
    routes_in,
    col,
    stage,
    recv,
    back,
    acc,
    ring,
    home,
    slot_of,
    weight_of,
    w_in,
    w_out,
    load_sem,
    given_send,
    given_recv,
    route_send,
    route_recv,
    z_send,
    z_recv,
    y_send,
    y_recv,
    att_send,
    att_recv,
    share_send,
    share_recv,
    own_sem,
    w_send,
    w_recv,
    col_send,
    col_recv,
    out_send,
    out_recv,
    back_send,
    back_recv,
    ring_send,
    ring_recv,
):
    z, y, x, c = (lax.axis_index(name) for name in MESH_AXES)
    model = residual.shape[1]
    wide = model // 2
    scale = math.log2(math.e) / math.sqrt(HD)

    cp = x * NC + c
    wrap = (z + 1) // NZ
    cp_ahead = lax.rem(cp + wrap, NX * NC)
    ahead = {"z": lax.rem(z + 1, NZ), "x": cp_ahead // NC, "c": lax.rem(cp_ahead, NC)}
    wrap = 1 - (z + NZ - 1) // NZ
    cp_behind = lax.rem(cp + NX * NC - wrap, NX * NC)
    behind = {
        "z": lax.rem(z + NZ - 1, NZ),
        "x": cp_behind // NC,
        "c": lax.rem(cp_behind, NC),
    }

    def along(axis, position, distance, size):
        return {axis: lax.rem(position + distance, size)}

    def peer(k):
        other_y, other_x = lax.rem(y + k // NX, NY), lax.rem(x + k % NX, NX)
        return {"y": other_y, "x": other_x}, other_y * NX + other_x

    barrier = pltpu.get_barrier_semaphore()

    def greet(k, carry):
        pl.semaphore_signal(barrier, inc=1, device_id=peer(k)[0], device_id_type=MESH)
        return carry

    lax.fori_loop(1, PLANE, greet, 0)
    others = [ahead, behind, {"c": 1 - c}]
    others += [along("z", z, d, NZ) for d in range(1, NZ)]
    for other in others:
        pl.semaphore_signal(barrier, inc=1, device_id=other, device_id_type=MESH)
    pl.semaphore_wait(barrier, PLANE - 1 + len(others))

    def remote(source, target, send, recv, device):
        return pltpu.make_async_remote_copy(
            src_ref=source,
            dst_ref=target,
            send_sem=send,
            recv_sem=recv,
            device_id=device,
            device_id_type=MESH,
        )

    def hop(g, number):
        source = window.at[g, (3 - number) * NY + y]
        target = window.at[g, (2 - number) * NY + y]
        return remote(
            source, target, z_send.at[g, number - 1], z_recv.at[g, number - 1], ahead
        )

    def to_row(g, plane, d):
        block = window.at[g, plane * NY + y]
        return remote(
            block,
            block,
            y_send.at[g, plane, d - 1],
            y_recv.at[g, plane, d - 1],
            along("y", y, d, NY),
        )

    def route_copy(d):
        return remote(
            routes_ref,
            routes_in.at[d],
            route_send.at[d],
            route_recv.at[d],
            along("z", z, d, NZ),
        )

    def rotated(n):
        return lax.rem(x + 1 + n, KVH)

    def first(n, carry):
        g = rotated(n)
        window[g, 2 * NY + y] = kv_ref[g]
        hop(g, 1).start()
        for d in range(1, NY):

            @pl.when(y + d < NY)
            def _():
                to_row(g, 2, d).start()

        return carry

    lax.fori_loop(0, KVH, first, 0)

    for d in range(1, NZ):
        route_copy(d).start()
    loads = [
        pltpu.make_async_copy(queries_hbm, queries, load_sem.at[0]),
        pltpu.make_async_copy(residual_hbm, residual, load_sem.at[1]),
        pltpu.make_async_copy(weight_hbm, weight.at[c], load_sem.at[2]),
        remote(weight_hbm, weight.at[c], given_send, given_recv, {"c": 1 - c}),
    ]
    for load in loads:
        load.start()

    def second(n, carry):
        g = rotated(n)
        hop(g, 1).wait_recv()
        hop(g, 2).start()
        for d in range(1, NY):
            to_row(g, 1, d).start()
        return carry

    lax.fori_loop(0, KVH, second, 0)

    keys_at = lax.broadcasted_iota(jnp.int32, (TOK, SPAN), 1)
    tokens_at = lax.broadcasted_iota(jnp.int32, (TOK, SPAN), 0) + DOC_MAX
    allowed = (key_docs_ref[...] == query_docs_ref[...]) & (keys_at <= tokens_at)
    bias[...] = jnp.where(allowed, 0.0, -1e30)

    middle = pl.ds(pl.multiple_of((NY - y) * TOK, TOK), NY * TOK)
    bias_middle[...] = bias[:, middle]

    def outer_block(b):
        return b + NY * ((y + b) // NY)

    for b in range(NY + 1):
        at = pl.ds(pl.multiple_of(outer_block(b) * TOK, TOK), TOK)
        bias_outer[:, b * TOK : (b + 1) * TOK] = bias[:, at]

    def third(n, carry):
        g = rotated(n)
        hop(g, 2).wait_recv()
        for d in range(1, NY):

            @pl.when(y + d >= NY)
            def _():
                to_row(g, 0, d).start()

        return carry

    lax.fori_loop(0, KVH, third, 0)

    weight_copies = []
    for n, (hbm, vmem) in enumerate(((w_in_hbm, w_in), (w_out_hbm, w_out))):
        own_part = pltpu.make_async_copy(hbm.at[0], vmem.at[c], own_sem.at[n])
        given = remote(hbm.at[0], vmem.at[c], w_send.at[n], w_recv.at[n], {"c": 1 - c})
        own_part.start()
        given.start()
        weight_copies += [own_part, given]

    for load in loads:
        load.wait()

    def attend_copy(n):
        g = rotated(n)
        return remote(
            attended.at[g], arrived.at[x], att_send.at[n], att_recv.at[n], {"x": g}
        )

    def source_of(n):
        return lax.rem(x + NX - 1 - n, NX)

    def share_copy(n):
        source = source_of(n)
        return remote(
            share.at[n], shares_in.at[n], share_send.at[n], share_recv.at[n], {"x": source}
        )

    step = 512

    def product(rows, columns):
        total = jnp.dot(rows[:, : HG * HD], weight[0, :, columns], preferred_element_type=jnp.float32)
        total += jnp.dot(rows[:, HG * HD :], weight[1, :, columns], preferred_element_type=jnp.float32)
        return total

    def project(n):
        attend_copy(n).wait_recv()
        rows = arrived[source_of(n)]

        def part(m, carry):
            columns = pl.ds(pl.multiple_of(m * step, step), step)
            share[n, :, columns] = product(rows, columns).astype(jnp.bfloat16)
            return carry

        lax.fori_loop(0, model // step, part, 0)
        share_copy(n).start()

    def two_queries(g, i):
        first_column = g * GROUP * HD + i * HD
        return jnp.concatenate(
            [queries[:, pl.ds(pl.multiple_of(first_column + k * HD, HD), HD)] for k in range(2)],
            axis=0,
        )

    def score(q, keys, added):
        scores = lax.dot_general(
            q, keys, (((1,), (1,)), ((), ())), preferred_element_type=jnp.float32
        )
        return scores.reshape(2, TOK, keys.shape[0]) * scale + added

    def weighted(exponent, values):
        rows = exponent.astype(jnp.bfloat16).reshape(2 * TOK, values.shape[0])
        total = jnp.dot(rows, values, preferred_element_type=jnp.float32)
        return total.reshape(2, TOK, HD)

    low_lanes = lax.broadcasted_iota(jnp.int32, (TOK, HD), 1) < HD // 2

    def middle_part(n, carry):
        g = rotated(n)
        for d in range(1, NY):
            to_row(g, 1, d).wait_recv()
        block = window[g, NY : 2 * NY].reshape(NY * TOK, 2 * HD)
        keys, values = block[:, :HD], block[:, HD:]
        for i in range(0, GROUP, 2):
            scores = score(two_queries(g, i), keys, bias_middle[...])
            top = jnp.max(scores, axis=-1, keepdims=True)
            exponent = jnp.exp2(scores - top)
            denominator = jnp.sum(exponent, axis=-1, keepdims=True)
            numerator = weighted(exponent, values)
            for k in range(2):
                rows = pl.ds(pl.multiple_of(lax.rem(g, 2) * TOK, TOK), TOK)
                home[g // 2, rows, (i + k) * HD : (i + k + 1) * HD] = numerator[k]
                stats[g, i + k] = jnp.where(low_lanes, top[k], denominator[k])
        return carry

    lax.fori_loop(0, KVH, middle_part, 0)

    def one_kv_head(n, carry):
        g = rotated(n)
        for d in range(1, NY):

            @pl.when(y >= d)
            def _():
                to_row(g, 2, d).wait_recv()

            @pl.when(y < d)
            def _():
                to_row(g, 0, d).wait_recv()

        blocks = [window[g, y + outer_block(b)] for b in range(NY + 1)]
        keys = jnp.concatenate([block[:, :HD] for block in blocks], axis=0)
        values = jnp.concatenate([block[:, HD:] for block in blocks], axis=0)
        for i in range(0, GROUP, 2):
            scores = score(two_queries(g, i), keys, bias_outer[...])
            rows = pl.ds(pl.multiple_of(lax.rem(g, 2) * TOK, TOK), TOK)
            before = [home[g // 2, rows, (i + k) * HD : (i + k + 1) * HD] for k in range(2)]
            before_top = jnp.stack([stats[g, i + k][:, :1] for k in range(2)])
            before_sum = jnp.stack([stats[g, i + k][:, HD // 2 : HD // 2 + 1] for k in range(2)])
            top = jnp.maximum(jnp.max(scores, axis=-1, keepdims=True), before_top)
            exponent = jnp.exp2(scores - top)
            factor = jnp.exp2(before_top - top)
            denominator = jnp.sum(exponent, axis=-1, keepdims=True) + factor * before_sum
            numerator = weighted(exponent, values) + factor * jnp.stack(before)
            result = (numerator / denominator).astype(jnp.bfloat16)
            for k in range(2):
                attended[g, :, (i + k) * HD : (i + k + 1) * HD] = result[k]

        @pl.when(n < NX - 1)
        def _():
            attend_copy(n).start()

        @pl.when(n > 0)
        def _():
            project(n - 1)

        return carry

    lax.fori_loop(0, KVH, one_kv_head, 0)

    mine = attended[x]

    def own_product(m, carry):
        columns = pl.ds(pl.multiple_of(m * step, step), step)
        own[:, columns] = product(mine, columns)
        return carry

    lax.fori_loop(0, model // step, own_product, 0)

    for n in range(NX - 1):
        share_copy(n).wait_recv()

    def normalize(m, carry):
        rows = pl.ds(pl.multiple_of(m * 32, 32), 32)
        summed = residual[rows].astype(jnp.float32) + own[rows]
        for n in range(NX - 1):
            summed += shares_in[n, rows].astype(jnp.float32)
        own[rows] = summed
        mean = jnp.mean(summed * summed, axis=-1, keepdims=True)
        normed = (summed * lax.rsqrt(mean + 1e-06) * gain_ref[...]).astype(jnp.bfloat16)
        col[0, rows] = normed[:, :wide]
        col[0, pl.ds(pl.multiple_of(TOK + m * 32, 32), 32)] = normed[:, wide:]
        return carry

    lax.fori_loop(0, TOK // 32, normalize, 0)

    place = y * NX + x
    right, left = lax.rem(z + 1, NZ), lax.rem(z + NZ - 1, NZ)

    def ring_copy(direction, n, side):
        source, target = (n - 1, n) if direction == 0 else ((NZ + 1 - n) % NZ, NZ - n)
        rows = pl.ds(side * TOK, TOK)
        return remote(
            col.at[source, rows],
            col.at[target, rows],
            col_send.at[direction, n - 1, side],
            col_recv.at[direction, n - 1, side],
            {"z": right if direction == 0 else left},
        )

    steps = [
        (n, side, direction)
        for n in range(1, 5)
        for side in range(2)
        for direction in range(2)
        if n < 4 or side == direction
    ]
    for n, side, direction in steps:
        if n == 1:
            ring_copy(direction, 1, side).start()

    def far_first(k):
        return (2 + k) * (1 - k // 2) + (3 - k) * (k // 2)

    def exchange(source, target, sends, recvs, r):
        def send(k, carry):
            device, expert = peer(far_first(k // NX) * NX + far_first(k % NX))
            remote(
                source.at[r, expert], target.at[r, place], sends.at[r], recvs.at[r], device
            ).start()
            return carry

        lax.fori_loop(0, PLANE - 1, send, 0)
        target[r, place] = source[r, place]

    def whole(source, target, sends, recvs, r):
        others = pl.ds(0, PLANE - 1)
        return remote(
            source.at[r, others], target.at[r, others], sends.at[r], recvs.at[r], {"c": c}
        )

    token = lax.broadcasted_iota(jnp.int32, (TOK, TOK), 0)
    earlier = (token < lax.broadcasted_iota(jnp.int32, (TOK, TOK), 1)).astype(jnp.bfloat16)
    expert_row = lax.broadcasted_iota(jnp.int32, (PLANE, TOK), 0) + z * PLANE
    expert_row = expert_row.astype(jnp.float32)
    slot_row = lax.rem(lax.broadcasted_iota(jnp.int32, (PLANE * 2 * CAP, TOK), 0), 2 * CAP)
    side_row = slot_row // CAP
    slot_row = lax.rem(slot_row, CAP).astype(jnp.float32)

    def slots(r):
        chosen = jnp.zeros((PLANE, TOK), jnp.float32)
        weight = jnp.zeros((PLANE, TOK), jnp.float32)
        for j in range(8):
            hit = routes_in[r, j : j + 1, :] == expert_row
            chosen = jnp.where(hit, 1.0, chosen)
            weight = jnp.where(hit, routes_in[r, 8 + j : 9 + j, :], weight)
        rank = jnp.dot(
            chosen.astype(jnp.bfloat16), earlier, preferred_element_type=jnp.float32
        )
        slot_of[r] = jnp.where(chosen > 0.0, jnp.minimum(rank, float(CAP)), float(CAP))
        weight_of[r] = weight

    def by_slot(values):
        rows = jnp.broadcast_to(values[:, None, :], (PLANE, 2 * CAP, TOK))
        return rows.reshape(PLANE * 2 * CAP, TOK)

    def taken(r):
        return by_slot(slot_of[r]) == slot_row

    def both_sides(values):
        low, high = jnp.where(side_row == 0, values, 0.0), jnp.where(side_row == 1, values, 0.0)
        return jnp.concatenate([low, high], axis=1)

    def dispatch(r):
        slots(r)
        pick = both_sides(jnp.where(taken(r), 1.0, 0.0)).astype(jnp.bfloat16)

        def select(n, carry):
            columns = pl.ds(pl.multiple_of(n * step, step), step)
            rows = jnp.dot(pick, col[r, :, columns], preferred_element_type=jnp.float32)
            stage[r, :, :, columns] = rows.reshape(PLANE, 2 * CAP, step).astype(jnp.bfloat16)
            return carry

        lax.fori_loop(0, wide // step, select, 0)
        exchange(stage, recv, out_send, out_recv, r)

    def expert(blocks):
        rows = []
        for r in blocks:
            whole(stage, recv, out_send, out_recv, r).wait_recv()
            came = recv[r].astype(jnp.float32).reshape(PLANE, 2, CAP, wide)
            sides = [came[:, side].reshape(PLANE * CAP, wide) for side in range(2)]
            rows.append(jnp.concatenate(sides, axis=1).astype(jnp.bfloat16))
        rows = jnp.concatenate(rows, axis=0) if len(rows) > 1 else rows[0]
        width = w_out.shape[1]
        acts = []
        for p in range(2):
            gate_up = jnp.dot(rows, w_in[p], preferred_element_type=jnp.float32)
            gate, up = gate_up[:, :width], gate_up[:, width:]
            acts.append((gate / (1.0 + jnp.exp(-gate)) * up).astype(jnp.bfloat16))

        def down(n, carry):
            sides = []
            for side in range(2):
                columns = pl.ds(pl.multiple_of(side * wide + n * step, step), step)
                total = jnp.dot(acts[0], w_out[0, :, columns], preferred_element_type=jnp.float32)
                total += jnp.dot(acts[1], w_out[1, :, columns], preferred_element_type=jnp.float32)
                sides.append(total.reshape(len(blocks), PLANE, 1, CAP, step))
            total = jnp.concatenate(sides, axis=2).reshape(len(blocks), PLANE, 2 * CAP, step)
            columns = pl.ds(pl.multiple_of(n * step, step), step)
            for i, r in enumerate(blocks):
                recv[r, :, :, columns] = total[i].astype(jnp.bfloat16)
            return carry

        lax.fori_loop(0, wide // step, down, 0)

    routes_in[0] = routes_ref[...]
    for d in range(1, NZ):
        route_copy(d).wait()

    dispatch(0)

    groups = [(0,), (1, 7), (2, 6), (3, 5), (4,)]
    for n in range(1, 5):
        for at, side, direction in steps:
            if at == n:
                ring_copy(direction, n, side).wait_recv()
                if (n + 1, side, direction) in steps:
                    ring_copy(direction, n + 1, side).start()
        for r in groups[n]:
            dispatch(r)
        if n == 1:
            for copy in weight_copies:
                copy.wait()
        expert(groups[n - 1])

    def give_back(n):
        for r in groups[n]:
            exchange(recv, back, back_send, back_recv, r)

    def sum_copy(direction, n, side):
        source, target = (n, n - 1) if direction == 0 else (NZ - n, NZ + 1 - n)
        rows = pl.ds(side * TOK, TOK)
        return remote(
            acc.at[source, rows],
            ring.at[target, rows],
            ring_send.at[direction, n - 1, side],
            ring_recv.at[direction, n - 1, side],
            {"z": left if direction == 0 else right},
        )

    def weigh(r, sums):
        spread = both_sides(jnp.where(taken(r), by_slot(weight_of[r]), 0.0))
        high = spread.astype(jnp.bfloat16)
        low = (spread - high.astype(jnp.float32)).astype(jnp.bfloat16)

        def part(n, carry):
            columns = pl.ds(pl.multiple_of(n * step, step), step)
            rows = back[r, :, :, columns].reshape(PLANE * 2 * CAP, step)
            total = jnp.zeros((2 * TOK, step), jnp.float32)
            for matrix in (high, low):
                total += lax.dot_general(
                    matrix, rows, (((0,), (0,)), ((), ())), preferred_element_type=jnp.float32
                )
            sums[:, columns] = total
            return carry

        lax.fori_loop(0, wide // step, part, 0)

    give_back(3)
    expert(groups[4])
    give_back(4)
    for n in (4, 3, 2, 1, 0):
        for k, r in enumerate(groups[n]):
            whole(recv, back, back_send, back_recv, r).wait_recv()
            weigh(r, home.at[k])
        if n == 0:
            break
        for at, side, direction in steps:
            if at != n:
                continue
            r = n if direction == 0 else NZ - n
            rows = pl.ds(side * TOK, TOK)
            total = home[0 if n == 4 else direction, rows]
            if (n + 1, side, direction) in steps:
                sum_copy(direction, n + 1, side).wait_recv()
                total += ring[r, rows].astype(jnp.float32)
            acc[r, rows] = total.astype(jnp.bfloat16)
            sum_copy(direction, n, side).start()
        if n >= 2:
            give_back(n - 2)

    for side in range(2):
        rows = pl.ds(side * TOK, TOK)
        columns = pl.ds(side * wide, wide)
        moe_sum = home[0, rows]
        for direction in range(2):
            sum_copy(direction, 1, side).wait_recv()
            moe_sum += ring[direction * NZ, rows].astype(jnp.float32)
        out_ref[:, columns] = (own[:, columns] + moe_sum).astype(jnp.bfloat16)

    for r in range(NZ):
        whole(stage, recv, out_send, out_recv, r).wait_send()
        whole(recv, back, back_send, back_recv, r).wait_send()
    for n, side, direction in steps:
        ring_copy(direction, n, side).wait_send()
        sum_copy(direction, n, side).wait_send()

    def drain(g, carry):
        for number in (1, 2):
            hop(g, number).wait_send()
        for d in range(1, NY):
            to_row(g, 1, d).wait_send()

            @pl.when(y + d < NY)
            def _():
                to_row(g, 2, d).wait_send()

            @pl.when(y + d >= NY)
            def _():
                to_row(g, 0, d).wait_send()

        return carry

    lax.fori_loop(0, KVH, drain, 0)
    for n in range(NX - 1):
        attend_copy(n).wait_send()
        share_copy(n).wait_send()


def layer(
    queries, kv, key_docs, query_docs, routes, residual, gain, out_weight, expert_in, expert_out
):
    model = residual.shape[1]
    vmem, hbm = pl.BlockSpec(memory_space=pltpu.VMEM), pl.BlockSpec(memory_space=pl.ANY)
    dma = pltpu.SemaphoreType.DMA
    half = HEADS * HD // NX
    bf16, f32 = jnp.bfloat16, jnp.float32
    slots = (NZ, PLANE, 2 * CAP, model // 2)
    blocks = (NZ, 2 * TOK, model // 2)
    return pl.pallas_call(
        layer_kernel,
        out_shape=jax.ShapeDtypeStruct(residual.shape, bf16),
        in_specs=[hbm, vmem, vmem, vmem, vmem, hbm, vmem, hbm, hbm, hbm],
        out_specs=vmem,
        scratch_shapes=[
            pltpu.VMEM(queries.shape, bf16),
            pltpu.VMEM(residual.shape, bf16),
            pltpu.VMEM((TOK, SPAN), f32),
            pltpu.VMEM((TOK, NY * TOK), f32),
            pltpu.VMEM((TOK, (NY + 1) * TOK), f32),
            pltpu.VMEM((KVH, GROUP, TOK, HD), f32),
            pltpu.VMEM((KVH, 3 * NY, TOK, 2 * HD), bf16),
            pltpu.VMEM((KVH, TOK, half), bf16),
            pltpu.VMEM((NX, TOK, half), bf16),
            pltpu.VMEM((NC,) + out_weight.shape, bf16),
            pltpu.VMEM((NX - 1, TOK, model), bf16),
            pltpu.VMEM((NX - 1, TOK, model), bf16),
            pltpu.VMEM((TOK, model), f32),
            pltpu.VMEM((NZ,) + routes.shape, f32),
            pltpu.VMEM(blocks, bf16),
            pltpu.VMEM(slots, bf16),
            pltpu.VMEM(slots, bf16),
            pltpu.VMEM(slots, bf16),
            pltpu.VMEM(blocks, bf16),
            pltpu.VMEM((NZ + 1,) + blocks[1:], bf16),
            pltpu.VMEM((2,) + blocks[1:], f32),
            pltpu.VMEM((NZ, PLANE, TOK), f32),
            pltpu.VMEM((NZ, PLANE, TOK), f32),
            pltpu.VMEM((2,) + expert_in.shape[1:], bf16),
            pltpu.VMEM((2,) + expert_out.shape[1:], bf16),
            dma((3,)),
            dma,
            dma,
            dma((NZ,)),
            dma((NZ,)),
            dma((KVH, 2)),
            dma((KVH, 2)),
            dma((KVH, 3, NY - 1)),
            dma((KVH, 3, NY - 1)),
            dma((NX - 1,)),
            dma((NX - 1,)),
            dma((NX - 1,)),
            dma((NX - 1,)),
            dma((2,)),
            dma((2,)),
            dma((2,)),
            dma((2, 4, 2)),
            dma((2, 4, 2)),
            dma((NZ,)),
            dma((NZ,)),
            dma((NZ,)),
            dma((NZ,)),
            dma((2, 4, 2)),
            dma((2, 4, 2)),
        ],
        compiler_params=pltpu.CompilerParams(
            collective_id=1, has_side_effects=True, vmem_limit_bytes=60 * 2**20
        ),
        cost_estimate=pl.CostEstimate(
            flops=14 * 10**9, bytes_accessed=20 * 2**20, transcendentals=HEADS * TOK * SPAN
        ),
        name="layer",
    )(queries, kv, key_docs, query_docs, routes, residual, gain, out_weight, expert_in, expert_out)


def on_device(
    queries,
    keyvals,
    residual,
    out_weight,
    norm_gain,
    doc_ids,
    expert_ids,
    route_weights,
    expert_in,
    expert_out,
):
    number = ((lax.axis_index("x") * NC + lax.axis_index("c")) * NZ + lax.axis_index("z")) * NY
    number += lax.axis_index("y")
    padded = jnp.concatenate([jnp.full((DOC_MAX,), -1, jnp.int32), doc_ids], axis=0)
    key_docs = lax.dynamic_slice_in_dim(padded, number * TOK, SPAN, 0)
    routes = jnp.concatenate([expert_ids.astype(jnp.float32), route_weights], axis=1).T
    return layer(
        queries,
        keyvals.transpose(1, 0, 2),
        key_docs[None, :],
        key_docs[DOC_MAX:, None],
        routes,
        residual,
        norm_gain[None],
        out_weight,
        expert_in,
        expert_out,
    )


def solution(mesh):
    torus = Mesh(mesh.devices.reshape(NZ, NY, NX, NC), ("z", "y", "x", "c"))
    tokens = ("x", "c", "z", "y")
    experts = ("z", "y", "x", "c")
    placed = (
        P(tokens, None),
        P(tokens, None, None),
        P(tokens, None),
        P(("x", "c"), None),
        P(),
        P(),
        P(tokens, None),
        P(tokens, None),
        P(experts, None, None),
        P(experts, None, None),
    )
    return jax.shard_map(
        on_device, mesh=torus, in_specs=placed, out_specs=P(tokens, None), check_vma=False
    )
```
